512 devices in a mesh: lat: 64 (over x, z), sec: 8 (over y, core).
Axes of the slice: x: 4, y: 4, z: 16, core: 2. Of those that a mesh axis runs over, the one named last changes fastest.
Arguments:
- velocity: float32 [256, 64, 1024], P('lat', 'sec'), may hold values from -3 to 3
- base_visc: float32 [256, 64, 1024], P('lat', 'sec'), may hold values from 0.5 to 5
- yielded: int32 [256, 64, 1024], P('lat', 'sec'), may hold values 0 or 1
- colors: int32 [256, 64, 1024], P('lat', 'sec'), may hold values from 0 to 7, as said below
- forcing: float32 [256, 64, 1024], P('lat', 'sec'), may hold values from -6 to 6
- block_diag: float32 [2, 128, 128], replicated, may hold values from -0.0625 to 0.0625
- block_below: float32 [2, 128, 128], replicated, may hold values from -0.0625 to 0.0625
- block_above: float32 [2, 128, 128], replicated, may hold values from -0.0625 to 0.0625
- weak_lines: int32 [8, 64, 64], P('sec', 'lat'), may hold values from 0 to 127, as said below
- weak_owner: int32 [8, 64, 64, 1], P('sec', 'lat'), may hold values from 0 to 63; in each aligned block of 64 rows (0 to 63, 64 to 127, ..., all dimensions but the last counted through in order) at most 4 rows name the same one
Outputs:
- correction: float32 [256, 64, 1024], P('lat', 'sec')
- weak_grad: float32 [64, 256], P('lat')
The draws below stay inside these ranges and needn't reach their ends.
Inputs may be any that keep to these rules, and one draw needn't show every extreme that they name: `colors`: no two cells of one stencil (a cell and its six face neighbours) share a color. `weak_lines`: the entries of one device are distinct lines of its pencil block, numbered q = 16 * (x - 8 * s) + (y - 16 * l). `weak_owner`: among the rows of one device no owner is named more than 4 times; in some device some owner is named exactly 4 times.
All inputs are finite; a program needn't handle non-finite values. No bound on the sum of `yielded` on one device may be relied on, other than what follows from the above.
Results may differ from the reference program's by a relative error of at most 0.0003.
Values sent between devices are 32-bit elements; how exact they have to be, the bound alone decides.
No kernel may reach another device: no remote copies, remote signals or barrier semaphores. Data moves between devices by JAX's collectives and lax.ppermute only.
A program may use at most 64 MiB of HBM per device.

```python
import math
import jax
import jax.numpy as jnp
import numpy as np
from jax import lax

RADIAL = 256
BLOCK = 128
TILE_X = 8
LINES_Y = 16
WEAK_ROWS = 64
SLOTS = 4
GRID_X = 64
GRID_Y = 1024
BLOCKS = 2
N_LAT = 64
N_SEC = 8


def draw_colors(key, part):
    key = jax.random.fold_in(key, 11)
    key_shift, key_split, key_extra, key_label = jax.random.split(key, 4)
    radial_index = jnp.arange(RADIAL, dtype=jnp.int32)[:, None, None]
    row_index = jnp.arange(GRID_X, dtype=jnp.int32)[None, :, None]
    col_index = jnp.arange(GRID_Y, dtype=jnp.int32)[None, None, :]
    offset = jax.random.randint(key_shift, (), 0, 7, dtype=jnp.int32)
    split_class = jax.random.randint(key_split, (), 0, 7, dtype=jnp.int32)
    klass = (radial_index + 2 * row_index + 3 * col_index + offset) % 7
    extra = jax.random.randint(key_extra, (RADIAL, GRID_X, GRID_Y), 0, 2, dtype=jnp.int32)
    label = jnp.where((klass == split_class) & (extra == 1), 7, klass)
    labels = jax.random.permutation(key_label, 8).astype(jnp.int32)
    return jnp.take(labels, label).astype(jnp.int32)


def draw_weak_lines(key, part):
    key = jax.random.fold_in(key, 23)
    device_keys = jax.random.split(key, N_SEC * N_LAT)

    def pick_lines(device_key):
        return jax.random.permutation(device_key, TILE_X * LINES_Y)[:WEAK_ROWS]
    picks = jax.vmap(pick_lines)(device_keys)
    return picks.reshape(N_SEC, N_LAT, WEAK_ROWS).astype(jnp.int32)


def set_ends(values, stream_key, low, top_value):
    dims = values.shape
    index_at = [jax.random.randint(jax.random.fold_in(stream_key, axis), (), 0, dims[axis]) for axis in range(len(dims))]
    values = values.at[tuple(index_at)].set(low)
    longest = dims.index(max(dims))
    index_at[longest] = (index_at[longest] + 1) % dims[longest]
    return values.at[tuple(index_at)].set(top_value)


def level_of(rng, shape, cuts, low, high):
    factor_of = 1.0
    for axis_at, parts in cuts:
        steps = jax.random.uniform(jax.random.fold_in(jax.random.fold_in(rng, 6), axis_at), (parts,), jnp.float32, low / len(cuts), high / len(cuts))
        factor_of = factor_of * jnp.repeat(jnp.exp(steps), shape[axis_at] // parts).reshape((-1,) + (1,) * (len(shape) - 1 - axis_at))
    return factor_of


def deal_out(rng, own, number, rows, number_of, top, most, skew):
    order = jax.random.permutation(rng, number_of)
    packed, usual = portions_of(number_of, rows * top, most, skew, True), portions_of(number_of, rows * top, most, skew, False)
    places = jnp.arange(number_of)

    def named(lengths, turn):
        used = int((lengths > 0).sum())
        fixed = max(1, used // 4)
        moved = fixed + (places - fixed + turn * (used - fixed)) % max(1, number_of - fixed)
        return jnp.zeros((number_of,), jnp.int32).at[order[jnp.where(places < fixed, places, moved)]].set(jnp.asarray(lengths, jnp.int32))

    lengths = jnp.where(number % 4 == 0, named(packed, number // 4), named(usual, number - number // 4 - 1))
    mixed = jax.random.permutation(jax.random.fold_in(own, 3), number_of)
    giver, receiver = mixed[0:number_of // 2 * 2:2], mixed[1:number_of // 2 * 2:2]
    margin = jnp.minimum(lengths[giver] - 1, most - lengths[receiver]) // 2
    margin = jnp.where((giver == order[0]) | (receiver == order[0]) | (lengths[receiver] == 0), 0, jnp.maximum(margin, 0))
    moved = jax.random.randint(jax.random.fold_in(own, 4), (number_of // 2,), 0, 1 << 20) % (margin + 1)
    lengths = lengths.at[giver].add(-moved).at[receiver].add(moved)
    members = jnp.searchsorted(jnp.cumsum(lengths), jnp.arange(rows * top), side="right").astype(jnp.int32)
    table = members.reshape(top, rows).T
    table = table[jax.random.permutation(jax.random.fold_in(own, 1), rows)]
    turn = jax.random.randint(jax.random.fold_in(own, 2), (rows, 1), 0, top)
    return jnp.take_along_axis(table, (jnp.arange(top)[None, :] + turn) % top, axis=1)


def portions_of(count, total, limit, slope, full):
    weights = [(1 << 20) // math.isqrt(grade ** slope) + 1 for grade in range(1, count + 1)]
    largest = limit if full else min(limit, max(-(-total // count), total * weights[0] // sum(weights)))
    least = 1 if total - largest >= count - 1 else 0
    counts, spare = [largest] + [least] * (count - 1), total - largest - least * (count - 1)
    while spare > 0:
        candidates = [i for i in range(1, count) if counts[i] < largest] or [i for i in range(1, count) if counts[i] < limit]
        whole, budget = sum([weights[i] for i in candidates]), spare
        for i in candidates:
            more = min(limit - counts[i], max(1, budget * weights[i] // whole), spare)
            counts[i] = counts[i] + more
            spare = spare - more
    return np.array(counts)


def centred(stream_key, extent, width, reach, shards=(), held_as=jnp.bfloat16):
    factor_of = level_of(stream_key, extent, shards, -0.22, 0.18) if shards else 1.0
    drawn = jax.random.normal(stream_key, extent, jnp.float32) * width * factor_of
    return jnp.minimum(jnp.maximum(drawn, -reach), reach).astype(held_as)


def setup_inputs(seed: int = 0) -> dict:
    key_of = jax.random.split(jax.random.key(seed), 11)
    velocity = centred(key_of[0], (RADIAL, GRID_X, GRID_Y), 0.5, 3.0, ((0, 64), (1, 8)), jnp.float32)
    base_visc = jnp.clip(jnp.exp(math.log(5.0) - 2.3025851 * jax.random.uniform(key_of[1], (RADIAL, GRID_X, GRID_Y), jnp.float32) ** level_of(key_of[1], (RADIAL, GRID_X, GRID_Y), ((0, 64), (1, 8)), -0.2, 0.2)), 0.5, 5.0)
    yielded = set_ends((jax.random.randint(key_of[2], (RADIAL, GRID_X, GRID_Y), 0, 3) < 1).astype(jnp.int32), jax.random.fold_in(key_of[2], 1), 0, 1)
    colors = draw_colors(jax.random.fold_in(key_of[10], 71), 0)
    forcing = centred(key_of[4], (RADIAL, GRID_X, GRID_Y), 1.0, 6.0, ((0, 64), (1, 8)), jnp.float32)
    block_diag = centred(key_of[5], (BLOCKS, BLOCK, BLOCK), (64 * BLOCK) ** -0.5, 0.0625, (), jnp.float32)
    block_below = centred(key_of[6], (BLOCKS, BLOCK, BLOCK), (64 * BLOCK) ** -0.5, 0.0625, (), jnp.float32)
    block_above = centred(key_of[7], (BLOCKS, BLOCK, BLOCK), (64 * BLOCK) ** -0.5, 0.0625, (), jnp.float32)
    weak_lines = draw_weak_lines(jax.random.fold_in(key_of[10], 71), 0)
    weak_owner_keys = jax.random.split(jax.random.fold_in(key_of[9], 1), N_SEC * N_LAT * WEAK_ROWS // WEAK_ROWS)
    weak_owner_turns = jax.random.permutation(jax.random.fold_in(key_of[9], 3), N_SEC * N_LAT * WEAK_ROWS // WEAK_ROWS)
    weak_owner = jax.vmap(lambda own, number: deal_out(jax.random.fold_in(key_of[9], 2), own, number, WEAK_ROWS, N_LAT, 1, SLOTS, 2))(weak_owner_keys, weak_owner_turns).reshape((N_SEC, N_LAT, WEAK_ROWS, 1))
    return dict(velocity=velocity, base_visc=base_visc, yielded=yielded, colors=colors, forcing=forcing, block_diag=block_diag, block_below=block_below, block_above=block_above, weak_lines=weak_lines, weak_owner=weak_owner)


FINITE_STEP = 0.03125
YIELD_WEIGHT = 0.25
NEIGHBOURS = ((2, 1, 1), (0, 1, 1), (1, 2, 1), (1, 0, 1), (1, 1, 2), (1, 1, 0))


def stencil(field_pad, visc_pad, base_visc, forcing):
    level_count, width_x, width_y = base_visc.shape
    centre = field_pad[1:-1, 1:-1, 1:-1]
    visc_mid = visc_pad[1:-1, 1:-1, 1:-1]
    flux_sum = jnp.zeros_like(centre)
    spread = jnp.zeros_like(centre)
    for shift_level, shift_row, shift_col in NEIGHBOURS:
        near_value = field_pad[shift_level:shift_level + level_count, shift_row:shift_row + width_x, shift_col:shift_col + width_y]
        near_visc = visc_pad[shift_level:shift_level + level_count, shift_row:shift_row + width_x, shift_col:shift_col + width_y]
        difference = centre - near_value
        flux_sum = flux_sum + 0.5 * (visc_mid + near_visc) * difference
        spread = spread + difference
    return flux_sum + base_visc * centre - forcing, 0.5 * visc_mid * spread


def apply_blocks(field, block_diag, block_below, block_above):
    block_count = block_diag.shape[0]
    block_width = block_diag.shape[1]
    blocks = field.reshape(block_count, block_width, -1)
    zero_block = jnp.zeros_like(blocks[:1])
    below_block = jnp.concatenate([zero_block, blocks[:-1]], axis=0)
    above_block = jnp.concatenate([blocks[1:], zero_block], axis=0)
    highest = lax.Precision.HIGHEST
    output = jnp.einsum("bij,bjk->bik", block_diag, blocks, precision=highest)
    output = output + jnp.einsum("bij,bjk->bik", block_below, below_block, precision=highest)
    output = output + jnp.einsum("bij,bjk->bik", block_above, above_block, precision=highest)
    return output.reshape(field.shape)


def band_product(diagonal, lower_band, upper_band, padded):
    return diagonal * padded[1:-1] + lower_band * padded[:-2] + upper_band * padded[2:]


def reference(velocity, base_visc, yielded, colors, forcing, block_diag, block_below, block_above, weak_lines, weak_owner):
    yield_coef = yielded.astype(jnp.float32) * YIELD_WEIGHT
    base_pad = jnp.pad(base_visc, 1)
    coef_pad = jnp.pad(yield_coef, 1)

    def evaluate(field_pad):
        visc_pad = base_pad / (1.0 + coef_pad * field_pad * field_pad)
        return stencil(field_pad, visc_pad, base_visc, forcing)

    residual, sensitivity = evaluate(jnp.pad(velocity, 1))
    colour_pad = jnp.pad(colors, ((1, 1), (0, 0), (0, 0)), constant_values=-1)
    below_colour = colour_pad[:-2]
    above_colour = colour_pad[2:]
    diagonal = jnp.zeros_like(residual)
    lower_band = jnp.zeros_like(residual)
    upper_band = jnp.zeros_like(residual)
    for colour_id in range(8):
        step_size = FINITE_STEP * (colour_id + 1)
        seed_mask = (colors == colour_id).astype(jnp.float32)
        shifted, unused = evaluate(jnp.pad(velocity + step_size * seed_mask, 1))
        column = (shifted - residual) / step_size
        diagonal = jnp.where(colors == colour_id, column, diagonal)
        lower_band = jnp.where(below_colour == colour_id, column, lower_band)
        upper_band = jnp.where(above_colour == colour_id, column, upper_band)
    initial = apply_blocks(residual, block_diag, block_below, block_above)
    radial_pad = jnp.pad(initial, ((1, 1), (0, 0), (0, 0)))
    remainder = residual - band_product(diagonal, lower_band, upper_band, radial_pad)
    correction = initial + apply_blocks(remainder, block_diag, block_below, block_above)
    gradient = correction * sensitivity
    sector_index = jnp.arange(N_SEC, dtype=jnp.int32)[:, None, None]
    lateral_index = jnp.arange(N_LAT, dtype=jnp.int32)[None, :, None]
    line_x = (sector_index * TILE_X + weak_lines // LINES_Y).reshape(-1)
    line_y = (lateral_index * LINES_Y + weak_lines % LINES_Y).reshape(-1)
    weak_rows = gradient[:, line_x, line_y]
    weak_grad = jax.ops.segment_sum(weak_rows.T, weak_owner.reshape(-1), num_segments=N_LAT)
    return correction, weak_grad
```

```python
import jax
import jax.numpy as jnp
from jax import lax
from jax.experimental import pallas as pl
from jax.experimental.pallas import tpu as pltpu
from jax.sharding import PartitionSpec as P

LANES = 128
ROWS = 8
FIELDS = 5
FINITE_STEP = 0.03125
YIELD_WEIGHT = 0.25
HIGHEST = lax.Precision.HIGHEST
VMEM = pl.BlockSpec(memory_space=pltpu.VMEM)
HBM = pl.BlockSpec(memory_space=pltpu.HBM)
MIB = 1024 * 1024


def viscosity(field, base, coef):
    return base / (1.0 + coef * field * field)


def rim_kernel(
    velocity_far,
    base_far,
    yielded_far,
    low_level,
    high_level,
    low_row,
    high_row,
    velocity,
    base,
    yielded,
    landed,
):
    arrays = ((velocity_far, velocity), (base_far, base), (yielded_far, yielded))
    copies = [pltpu.make_async_copy(far, near, landed.at[place]) for place, (far, near) in enumerate(arrays)]
    for copy in copies:
        copy.start()
    for copy in copies:
        copy.wait()
    levels = velocity.shape[0]
    rows = velocity.shape[1]
    for level in range(levels):
        v = velocity[level]
        eta = viscosity(v, base[level], yielded[level].astype(jnp.float32) * YIELD_WEIGHT)
        low_row[0, level, :] = v[0]
        low_row[1, level, :] = eta[0]
        high_row[0, level, :] = v[rows - 1]
        high_row[1, level, :] = eta[rows - 1]
        if level == 0:
            low_level[0] = v
            low_level[1] = eta
        if level == levels - 1:
            high_level[0] = v
            high_level[1] = eta


def turns():
    width = LANES // ROWS
    row = lax.broadcasted_iota(jnp.int32, (ROWS, LANES), 0)
    lane = lax.broadcasted_iota(jnp.int32, (ROWS, LANES), 1)
    return (lane // width - row) & (ROWS - 1), (lane + row * width) & (LANES - 1)


def to_lines(block, fetch):
    skewed = pltpu.roll(block, 0, 1, stride=LANES // ROWS, stride_axis=0)
    return jnp.take_along_axis(skewed, fetch[0], axis=0, mode="promise_in_bounds")


def to_cells(block, fetch):
    skewed = jnp.take_along_axis(block, fetch[0], axis=0, mode="promise_in_bounds")
    return jnp.take_along_axis(skewed, fetch[1], axis=1, mode="promise_in_bounds")


def tile_kernel(velocity, base, yielded, colors, forcing, below, above, left, right, out):
    levels, rows, width = velocity.shape
    fetch = turns()
    lane = lax.broadcasted_iota(jnp.int32, (rows, width), 1)
    row = lax.broadcasted_iota(jnp.int32, (rows, width), 0)
    fields = [below[0]] + [velocity[level] for level in range(levels)] + [above[0]]
    coefs = [yielded[level].astype(jnp.float32) * YIELD_WEIGHT for level in range(levels)]
    inverse = [
        1.0 / (1.0 + coefs[level] * fields[level + 1] * fields[level + 1]) for level in range(levels)
    ]
    etas = [below[1]] + [base[level] * inverse[level] for level in range(levels)] + [above[1]]

    def neighbours(centre, side, level):
        low_x = jnp.where(row == 0, left[side, level][None, :], pltpu.roll(centre, 1, 0))
        high_x = jnp.where(row == rows - 1, right[side, level][None, :], pltpu.roll(centre, rows - 1, 0))
        low_y = jnp.where(lane == 0, 0.0, pltpu.roll(centre, 1, 1))
        high_y = jnp.where(lane == width - 1, 0.0, pltpu.roll(centre, width - 1, 1))
        return low_x, high_x, low_y, high_y

    for level in range(levels):
        v = fields[level + 1]
        eta = etas[level + 1]
        b = base[level]
        coef = coefs[level]
        near_v = neighbours(v, 0, level) + (fields[level], fields[level + 2])
        near_eta = neighbours(eta, 1, level) + (etas[level], etas[level + 2])
        value_sum = near_v[0]
        eta_sum = near_eta[0]
        product_sum = near_v[0] * near_eta[0]
        for near_value, near_visc in zip(near_v[1:], near_eta[1:]):
            value_sum = value_sum + near_value
            eta_sum = eta_sum + near_visc
            product_sum = product_sum + near_value * near_visc
        spread = 6.0 * v - value_sum
        sensitivity = 0.5 * eta * spread
        residual = sensitivity + 0.5 * (v * eta_sum - product_sum) + b * v - forcing[level]
        step = FINITE_STEP * (colors[level] + 1).astype(jnp.float32)
        moved = v + step
        moved_inverse = 1.0 / (1.0 + coef * moved * moved)
        moved_eta = b * moved_inverse
        slope = -coef * (moved + v) * eta * moved_inverse
        diagonal = 0.5 * eta_sum + 3.0 * moved_eta + 0.5 * slope * spread + b
        onto_below = 0.5 * (slope * (fields[level] - v) - etas[level] - moved_eta)
        onto_above = 0.5 * (slope * (fields[level + 2] - v) - etas[level + 2] - moved_eta)
        for place, field in enumerate((residual, diagonal, onto_below, onto_above, sensitivity)):
            for block in range(width // LANES):
                lines = to_lines(field[:, block * LANES : (block + 1) * LANES], fetch)
                start = block * ROWS * FIELDS * levels + place * levels + level
                out[pl.ds(start, ROWS, stride=FIELDS * levels), :] = lines


def lines_kernel(line_ids, owner_ids, lines_of):
    entries = line_ids.shape[1]
    owner_count, line_count = lines_of.shape
    picks = (lax.broadcasted_iota(jnp.int32, (line_count, entries), 0) == line_ids[...]).astype(jnp.float32)
    owners = (lax.broadcasted_iota(jnp.int32, (owner_count, entries), 0) == owner_ids[...]).astype(jnp.float32)
    lines_of[...] = lax.dot_general(
        owners, picks, (((1,), (1,)), ((), ())), preferred_element_type=jnp.float32
    )


def pencil_kernel(levels, received, block_diag, block_below, block_above, lines_of, out, work):
    radial = work.shape[1]
    devices = radial // levels
    stride = FIELDS * levels
    for place in range(FIELDS):
        for level in range(levels):
            for group in range(devices // ROWS):
                work[place, pl.ds(group * ROWS * levels + level, ROWS, stride=levels), :] = received[
                    pl.ds(group * ROWS * stride + place * levels + level, ROWS, stride=stride), :
                ]
    residual = work[0]
    half = radial // 2

    def apply_blocks(field):
        head, tail = field[:half], field[half:]
        first = jnp.dot(block_diag[0], head, precision=HIGHEST, preferred_element_type=jnp.float32)
        first = first + jnp.dot(block_above[0], tail, precision=HIGHEST, preferred_element_type=jnp.float32)
        second = jnp.dot(block_diag[1], tail, precision=HIGHEST, preferred_element_type=jnp.float32)
        second = second + jnp.dot(block_below[1], head, precision=HIGHEST, preferred_element_type=jnp.float32)
        return jnp.concatenate([first, second], axis=0)

    initial = apply_blocks(residual)
    level_index = lax.broadcasted_iota(jnp.int32, (radial, LANES), 0)
    from_above = jnp.where(level_index == radial - 1, 0.0, pltpu.roll(work[2] * initial, radial - 1, 0))
    from_below = jnp.where(level_index == 0, 0.0, pltpu.roll(work[3] * initial, 1, 0))
    remainder = residual - (work[1] * initial + from_above + from_below)
    correction = initial + apply_blocks(remainder)
    gradient = correction * work[4]

    owned = lax.dot_general(
        lines_of[...],
        gradient,
        (((1,), (1,)), ((), ())),
        precision=HIGHEST,
        preferred_element_type=jnp.float32,
    )
    work[0] = correction
    parts = radial // LANES
    back = levels + parts
    for group in range(devices // ROWS):
        for level in range(levels):
            out[pl.ds(group * ROWS * back + level, ROWS, stride=back), :] = work[
                0, pl.ds(group * ROWS * levels + level, ROWS, stride=levels), :
            ]
        for part in range(parts):
            out[pl.ds(group * ROWS * back + levels + part, ROWS, stride=back), :] = owned[
                group * ROWS : (group + 1) * ROWS, part * LANES : (part + 1) * LANES
            ]


def owned_kernel(levels, received, owned):
    sectors, _, radial = owned.shape
    parts = radial // LANES
    back = levels + parts
    groups = received.shape[0] // (back * ROWS)
    for part in range(parts):
        total = received[pl.ds(levels + part, ROWS, stride=back), :]
        for group in range(1, groups):
            total = total + received[pl.ds(group * ROWS * back + levels + part, ROWS, stride=back), :]
        total = jnp.sum(total, axis=0, keepdims=True)
        for sector in range(sectors):
            owned[sector, :, part * LANES : (part + 1) * LANES] = total


def finish_kernel(received, correction):
    levels, rows, width = correction.shape
    groups = width // LANES
    back = received.shape[0] // (groups * ROWS)
    fetch = turns()
    for level in range(levels):
        for group in range(groups):
            lines = received[pl.ds(group * ROWS * back + level, ROWS, stride=back), :]
            correction[level, :, group * LANES : (group + 1) * LANES] = to_cells(lines, fetch)


def shifted(cells, axis, step):
    count = lax.axis_size(axis)
    return lax.ppermute(cells, axis, [(i, i + step) for i in range(count) if 0 <= i + step < count])


def swapped(rows, parts):
    devices = lax.axis_size("lat")
    sent = rows.reshape(devices, -1, parts, LANES)
    taken = lax.all_to_all(sent, "lat", split_axis=0, concat_axis=0, tiled=True)
    return taken.reshape(rows.shape)


def kernel_call(body, shapes, count, flops, name, scratch=(), place=VMEM, grant=32):
    total = sum(4 * size for size in flops[1:])
    return pl.pallas_call(
        body,
        out_shape=shapes,
        in_specs=[place] * count,
        out_specs=[VMEM] * len(shapes),
        scratch_shapes=scratch,
        compiler_params=pltpu.CompilerParams(vmem_limit_bytes=grant * MIB),
        cost_estimate=pl.CostEstimate(flops=flops[0], bytes_accessed=total, transcendentals=0),
        name=name,
    )


def f32(*shape):
    return jax.ShapeDtypeStruct(shape, jnp.float32)


def local(
    velocity,
    base_visc,
    yielded,
    colors,
    forcing,
    block_diag,
    block_below,
    block_above,
    weak_lines,
    weak_owner,
):
    levels, rows, width = velocity.shape
    devices = lax.axis_size("lat")
    sectors = lax.axis_size("sec")
    radial = levels * devices
    cells = levels * rows * width
    level_rim = f32(2, rows, width)
    row_rim = f32(2, levels, width)
    low_level, high_level, low_row, high_row = kernel_call(
        rim_kernel,
        [level_rim, level_rim, row_rim, row_rim],
        3,
        (4 * cells, 4 * cells),
        "rim",
        [
            pltpu.VMEM(velocity.shape, jnp.float32),
            pltpu.VMEM(velocity.shape, jnp.float32),
            pltpu.VMEM(velocity.shape, jnp.int32),
            pltpu.SemaphoreType.DMA((3,)),
        ],
        HBM,
        60,
    )(velocity, base_visc, yielded)
    left = shifted(high_row, "sec", 1)
    right = shifted(low_row, "sec", -1)
    below = shifted(high_level, "lat", 1)
    above = shifted(low_level, "lat", -1)
    (fields,) = kernel_call(
        tile_kernel,
        [f32(devices * FIELDS * levels, LANES)],
        9,
        (60 * cells, 12 * cells),
        "tile",
    )(velocity, base_visc, yielded, colors, forcing, below, above, left, right)
    fields = swapped(fields, levels)
    back = levels + radial // LANES

    picked = weak_lines.reshape(1, -1)
    line_width = LANES // rows
    place = (lax.axis_index("lat") + picked // line_width) % rows
    line_ids = place * line_width + picked % line_width

    (lines_of,) = kernel_call(
        lines_kernel, [f32(devices, LANES)], 2, (2 * devices * LANES * 64, devices * LANES), "lines"
    )(line_ids, weak_owner.reshape(1, -1))

    def pencil_body(*refs):
        pencil_kernel(levels, *refs)

    (improved,) = kernel_call(
        pencil_body,
        [f32(devices * back, LANES)],
        5,
        (24 * radial * radial * LANES, 12 * radial * LANES),
        "pencil",
        [pltpu.VMEM((FIELDS, radial, LANES), jnp.float32)],
    )(
        fields,
        block_diag,
        block_below,
        block_above,
        lines_of,
    )
    improved = swapped(improved, 2)

    def owned_body(*refs):
        owned_kernel(levels, *refs)

    (owned,) = kernel_call(
        owned_body, [f32(sectors, 1, radial)], 1, (devices * radial, devices * radial), "owned"
    )(improved)
    sums = lax.all_to_all(owned, "sec", split_axis=0, concat_axis=0, tiled=True)
    (correction,) = kernel_call(
        finish_kernel, [f32(levels, rows, width)], 1, (4 * cells, 3 * cells), "finish"
    )(improved)
    weak_grad = jnp.sum(sums, axis=0)
    return (correction, weak_grad)


def solution(mesh):
    return jax.shard_map(
        local,
        mesh=mesh,
        in_specs=(
            P("lat", "sec", None),
            P("lat", "sec", None),
            P("lat", "sec", None),
            P("lat", "sec", None),
            P("lat", "sec", None),
            P(),
            P(),
            P(),
            P("sec", "lat", None),
            P("sec", "lat", None, None),
        ),
        out_specs=(P("lat", "sec", None), P("lat", None)),
        check_vma=False,
    )
```

```python
import jax
import jax.numpy as jnp
from jax import lax
from jax.experimental import pallas as pl
from jax.experimental.pallas import tpu as pltpu
from jax.sharding import PartitionSpec as P

LANES = 128
ROWS = 8
WIDTH = LANES // ROWS
FIELDS = 5
SENT = FIELDS + 1
FINITE_STEP = 0.03125
YIELD_WEIGHT = 0.25
HIGHEST = lax.Precision.HIGHEST
VMEM = pl.BlockSpec(memory_space=pltpu.VMEM)
HBM = pl.BlockSpec(memory_space=pltpu.HBM)
SMEM = pl.BlockSpec(memory_space=pltpu.SMEM)
MIB = 1024 * 1024


def places():
    row = lax.broadcasted_iota(jnp.int32, (ROWS, LANES), 0)
    lane = lax.broadcasted_iota(jnp.int32, (ROWS, LANES), 1)
    return row, lane // WIDTH, lane % WIDTH


def along_lane(block, row_of):
    return jnp.take_along_axis(block, row_of, axis=0, mode="promise_in_bounds")


def along_row(block, lane_of):
    return jnp.take_along_axis(block, lane_of, axis=1, mode="promise_in_bounds")


def to_lines(block, row_of):
    return along_lane(pltpu.roll(block, 0, 1, stride=WIDTH, stride_axis=0), row_of)


def cells_kernel(
    velocity_far,
    base_far,
    yielded_far,
    colors_far,
    forcing_far,
    cells,
    low_row,
    high_row,
    velocity,
    base,
    yielded,
    colors,
    landed,
):
    forcing = cells.at[FIELDS - 1]
    arrays = (
        (velocity_far, velocity),
        (base_far, base),
        (yielded_far, yielded),
        (colors_far, colors),
        (forcing_far, forcing),
    )
    copies = [pltpu.make_async_copy(far, near, landed.at[place]) for place, (far, near) in enumerate(arrays)]
    for copy in copies:
        copy.start()
    for copy in copies:
        copy.wait()
    levels, rows, _ = velocity.shape
    for level in range(levels):
        v = velocity[level]
        b = base[level]
        coef = yielded[level].astype(jnp.float32) * YIELD_WEIGHT
        eta = b / (1.0 + coef * v * v)
        cells[0, level] = v
        cells[1, level] = b
        cells[2, level] = coef
        cells[3, level] = FINITE_STEP * (colors[level] + 1).astype(jnp.float32)
        cells[FIELDS, level] = eta
        low_row[0, level, :] = v[0]
        low_row[1, level, :] = eta[0]
        high_row[0, level, :] = v[rows - 1]
        high_row[1, level, :] = eta[rows - 1]


def tile_kernel(cells, lines):
    _, levels, _, width = cells.shape
    row, group, _ = places()
    row_of = (group - row) & (ROWS - 1)
    for field in range(FIELDS):
        for level in range(levels):
            for block in range(width // LANES):
                lines[field, level, block] = to_lines(
                    cells[field, level, :, block * LANES : (block + 1) * LANES], row_of
                )


def rim_kernel(lines, cells, left, right, out):
    _, levels, _, width = cells.shape
    stride = SENT * levels
    blocks = width // LANES
    row, group, place = places()
    row_of = (group - row) & (ROWS - 1)
    lane = group * WIDTH + place
    low_lane = (((group - 1) & (ROWS - 1)) * WIDTH - 1) & (LANES - 1)
    high_lane = (((group - 2) & (ROWS - 1)) * WIDTH + WIDTH) & (LANES - 1)
    x_of = place & (ROWS - 1)
    for level in range(levels):
        for block in range(blocks):
            start = block * ROWS * stride + level
            for field in range(FIELDS):
                out[pl.ds(start + field * levels, ROWS, stride=stride), :] = lines[field, level, block]
            span = slice(block * LANES, (block + 1) * LANES)
            ends = jnp.where(
                row == 0,
                left[0, level, span][None, :],
                jnp.where(
                    row == 7,
                    right[0, level, span][None, :],
                    jnp.where(row == 4, left[1, level, span][None, :], right[1, level, span][None, :]),
                ),
            )
            lows = []
            highs = []
            for kind in (0, FIELDS):
                here = cells[kind, level, :, span]
                low = here
                high = here
                if block > 0:
                    before = cells[kind, level, :, slice((block - 1) * LANES, block * LANES)]
                    low = jnp.where(lane == LANES - 1, before, here)
                else:
                    low = jnp.where(lane == LANES - 1, 0.0, here)
                if block < blocks - 1:
                    after = cells[kind, level, :, slice((block + 1) * LANES, (block + 2) * LANES)]
                    high = jnp.where(lane == 0, after, here)
                else:
                    high = jnp.where(lane == 0, 0.0, here)
                lows.append(along_row(low, low_lane))
                highs.append(along_row(high, high_lane))
            low = along_lane(jnp.where(place < ROWS, lows[0], lows[1]), x_of)
            high = along_lane(jnp.where(place < ROWS, highs[0], highs[1]), x_of)
            slot = row_of
            whole = jnp.where(slot == 1, low, jnp.where(slot == 2, high, to_lines(ends, row_of)))
            out[pl.ds(start + FIELDS * levels, ROWS, stride=stride), :] = whole


def lines_kernel(line_ids, owner_ids, lines_of):
    entries = line_ids.shape[1]
    owner_count, line_count = lines_of.shape
    picks = (lax.broadcasted_iota(jnp.int32, (line_count, entries), 0) == line_ids[...]).astype(jnp.float32)
    owners = (lax.broadcasted_iota(jnp.int32, (owner_count, entries), 0) == owner_ids[...]).astype(jnp.float32)
    lines_of[...] = lax.dot_general(
        owners, picks, (((1,), (1,)), ((), ())), preferred_element_type=jnp.float32
    )


def pencil_kernel(
    levels,
    received,
    turn,
    block_diag,
    block_below,
    block_above,
    lines_of,
    out,
    work,
    velocity,
    viscosity,
):
    radial = work.shape[1]
    devices = radial // levels
    stride = SENT * levels
    velocity[pl.ds(0, ROWS), :] = jnp.zeros((ROWS, LANES), jnp.float32)
    velocity[pl.ds(radial + ROWS, ROWS), :] = jnp.zeros((ROWS, LANES), jnp.float32)
    viscosity[pl.ds(0, ROWS), :] = jnp.zeros((ROWS, LANES), jnp.float32)
    viscosity[pl.ds(radial + ROWS, ROWS), :] = jnp.zeros((ROWS, LANES), jnp.float32)
    for place in range(SENT):
        for level in range(levels):
            for group in range(devices // ROWS):
                rows = received[pl.ds(group * ROWS * stride + place * levels + level, ROWS, stride=stride), :]
                target = group * ROWS * levels + level
                if place == 0:
                    velocity[pl.ds(ROWS + target, ROWS, stride=levels), :] = rows
                else:
                    work[place, pl.ds(target, ROWS, stride=levels), :] = rows
    for start in range(0, radial, ROWS):
        v = velocity[pl.ds(ROWS + start, ROWS), :]
        viscosity[pl.ds(ROWS + start, ROWS), :] = work[1, pl.ds(start, ROWS), :] / (
            1.0 + work[2, pl.ds(start, ROWS), :] * v * v
        )

    _, group, place = places()
    shift = turn[0, 0]
    x = (group - shift) & (ROWS - 1)
    first_x, last_x = x == 0, x == ROWS - 1
    first_y, last_y = place == 0, place == WIDTH - 1
    side = jnp.where(first_y, (shift + 1) & (ROWS - 1), (shift + 2) & (ROWS - 1))
    v_lane = side * WIDTH + x
    eta_lane = v_lane + ROWS

    def lateral(block, x_rim, y_rim):
        return (
            jnp.where(first_x, x_rim, pltpu.roll(block, WIDTH, 1)),
            jnp.where(last_x, x_rim, pltpu.roll(block, LANES - WIDTH, 1)),
            jnp.where(first_y, y_rim, pltpu.roll(block, 1, 1)),
            jnp.where(last_y, y_rim, pltpu.roll(block, LANES - 1, 1)),
        )

    for start in range(0, radial, ROWS):
        here = pl.ds(start, ROWS)
        v = velocity[pl.ds(ROWS + start, ROWS), :]
        v_low = velocity[pl.ds(ROWS + start - 1, ROWS), :]
        v_high = velocity[pl.ds(ROWS + start + 1, ROWS), :]
        eta = viscosity[pl.ds(ROWS + start, ROWS), :]
        eta_low = viscosity[pl.ds(ROWS + start - 1, ROWS), :]
        eta_high = viscosity[pl.ds(ROWS + start + 1, ROWS), :]
        b, coef, step, forcing = (work[field, here, :] for field in range(1, FIELDS))
        rim = work[FIELDS, here, :]
        near_v = lateral(v, rim, along_row(rim, v_lane)) + (v_low, v_high)
        near_eta = lateral(eta, pltpu.roll(rim, LANES // 2, 1), along_row(rim, eta_lane)) + (eta_low, eta_high)
        value_sum = near_v[0]
        eta_sum = near_eta[0]
        product_sum = near_v[0] * near_eta[0]
        for near_value, near_visc in zip(near_v[1:], near_eta[1:]):
            value_sum = value_sum + near_value
            eta_sum = eta_sum + near_visc
            product_sum = product_sum + near_value * near_visc
        spread = 6.0 * v - value_sum
        sensitivity = 0.5 * eta * spread
        moved = v + step
        moved_inverse = 1.0 / (1.0 + coef * moved * moved)
        moved_eta = b * moved_inverse
        slope = -coef * (moved + v) * eta * moved_inverse
        work[0, here, :] = sensitivity + 0.5 * (v * eta_sum - product_sum) + b * v - forcing
        work[1, here, :] = 0.5 * eta_sum + 3.0 * moved_eta + 0.5 * slope * spread + b
        work[2, here, :] = 0.5 * (slope * (v_low - v) - eta_low - moved_eta)
        work[3, here, :] = 0.5 * (slope * (v_high - v) - eta_high - moved_eta)
        work[4, here, :] = sensitivity

    residual = work[0]
    half = radial // 2

    def apply_blocks(field):
        head, tail = field[:half], field[half:]
        first = jnp.dot(block_diag[0], head, precision=HIGHEST, preferred_element_type=jnp.float32)
        first = first + jnp.dot(block_above[0], tail, precision=HIGHEST, preferred_element_type=jnp.float32)
        second = jnp.dot(block_diag[1], tail, precision=HIGHEST, preferred_element_type=jnp.float32)
        second = second + jnp.dot(block_below[1], head, precision=HIGHEST, preferred_element_type=jnp.float32)
        return jnp.concatenate([first, second], axis=0)

    initial = apply_blocks(residual)
    level_index = lax.broadcasted_iota(jnp.int32, (radial, LANES), 0)
    from_above = jnp.where(level_index == radial - 1, 0.0, pltpu.roll(work[2] * initial, radial - 1, 0))
    from_below = jnp.where(level_index == 0, 0.0, pltpu.roll(work[3] * initial, 1, 0))
    remainder = residual - (work[1] * initial + from_above + from_below)
    correction = initial + apply_blocks(remainder)
    gradient = correction * work[4]
    owned = lax.dot_general(
        lines_of[...],
        gradient,
        (((1,), (1,)), ((), ())),
        precision=HIGHEST,
        preferred_element_type=jnp.float32,
    )
    work[0] = correction
    parts = radial // LANES
    back = levels + parts
    for block in range(devices // ROWS):
        for level in range(levels):
            out[pl.ds(block * ROWS * back + level, ROWS, stride=back), :] = work[
                0, pl.ds(block * ROWS * levels + level, ROWS, stride=levels), :
            ]
        for part in range(parts):
            out[pl.ds(block * ROWS * back + levels + part, ROWS, stride=back), :] = owned[
                block * ROWS : (block + 1) * ROWS, part * LANES : (part + 1) * LANES
            ]


def owned_kernel(levels, received, owned):
    sectors, _, radial = owned.shape
    parts = radial // LANES
    back = levels + parts
    blocks = received.shape[0] // (back * ROWS)
    for part in range(parts):
        total = received[pl.ds(levels + part, ROWS, stride=back), :]
        for block in range(1, blocks):
            total = total + received[pl.ds(block * ROWS * back + levels + part, ROWS, stride=back), :]
        total = jnp.sum(total, axis=0, keepdims=True)
        for sector in range(sectors):
            owned[sector, :, part * LANES : (part + 1) * LANES] = total


def finish_kernel(received, correction):
    levels, rows, width = correction.shape
    blocks = width // LANES
    back = received.shape[0] // (blocks * ROWS)
    row, group, place = places()
    row_of = (group - row) & (ROWS - 1)
    lane_of = ((group + row) & (ROWS - 1)) * WIDTH + place
    for level in range(levels):
        for block in range(blocks):
            lines = received[pl.ds(block * ROWS * back + level, ROWS, stride=back), :]
            correction[level, :, block * LANES : (block + 1) * LANES] = along_row(
                along_lane(lines, row_of), lane_of
            )


def shifted(cells, axis, step):
    count = lax.axis_size(axis)
    return lax.ppermute(cells, axis, [(i, i + step) for i in range(count) if 0 <= i + step < count])


def swapped(rows, parts):
    devices = lax.axis_size("lat")
    sent = rows.reshape(devices, -1, parts, LANES)
    taken = lax.all_to_all(sent, "lat", split_axis=0, concat_axis=0, tiled=True)
    return taken.reshape(rows.shape)


def kernel_call(body, shapes, specs, work, name, scratch=()):
    return pl.pallas_call(
        body,
        out_shape=shapes,
        in_specs=specs,
        out_specs=[VMEM] * len(shapes),
        scratch_shapes=scratch,
        compiler_params=pltpu.CompilerParams(vmem_limit_bytes=32 * MIB),
        cost_estimate=pl.CostEstimate(flops=work[0], bytes_accessed=4 * work[1], transcendentals=0),
        name=name,
    )


def f32(*shape):
    return jax.ShapeDtypeStruct(shape, jnp.float32)


def local(
    velocity,
    base_visc,
    yielded,
    colors,
    forcing,
    block_diag,
    block_below,
    block_above,
    weak_lines,
    weak_owner,
):
    levels, rows, width = velocity.shape
    devices = lax.axis_size("lat")
    sectors = lax.axis_size("sec")
    radial = levels * devices
    cell_count = levels * rows * width
    row_shape = f32(2, levels, width)
    tile = (levels, rows, width)
    placed = f32(FIELDS, levels, width // LANES, ROWS, LANES)
    far = [
        pltpu.with_memory_space_constraint(array, pltpu.HBM)
        for array in (velocity, base_visc, yielded, colors, forcing)
    ]
    cells, low_row, high_row = kernel_call(
        cells_kernel,
        [f32(SENT, *tile), row_shape, row_shape],
        [HBM] * FIELDS,
        (20 * cell_count, 12 * cell_count),
        "cells",
        [pltpu.VMEM(tile, array.dtype) for array in far[:-1]] + [pltpu.SemaphoreType.DMA((FIELDS,))],
    )(*far)
    left = shifted(high_row, "sec", 1)
    right = shifted(low_row, "sec", -1)
    (lines,) = kernel_call(tile_kernel, [placed], [VMEM], (20 * cell_count, 10 * cell_count), "tile")(cells)
    (lines,) = kernel_call(
        rim_kernel,
        [f32(devices * SENT * levels, LANES)],
        [VMEM] * 4,
        (20 * cell_count, 12 * cell_count),
        "rims",
    )(lines, cells, left, right)
    lines = swapped(lines, levels)

    picked = weak_lines.reshape(1, -1)
    turn = lax.axis_index("lat") & (rows - 1)
    place = (turn + picked // WIDTH) & (rows - 1)
    line_ids = place * WIDTH + picked % WIDTH
    (lines_of,) = kernel_call(
        lines_kernel,
        [f32(devices, LANES)],
        [VMEM] * 2,
        (2 * devices * LANES * 64, devices * LANES),
        "lines",
    )(line_ids, weak_owner.reshape(1, -1))
    back = levels + radial // LANES

    def pencil_body(*refs):
        pencil_kernel(levels, *refs)

    (improved,) = kernel_call(
        pencil_body,
        [f32(devices * back, LANES)],
        [VMEM, SMEM, VMEM, VMEM, VMEM, VMEM],
        (24 * radial * radial * LANES, 12 * radial * LANES),
        "pencil",
        [
            pltpu.VMEM((SENT, radial, LANES), jnp.float32),
            pltpu.VMEM((radial + 2 * ROWS, LANES), jnp.float32),
            pltpu.VMEM((radial + 2 * ROWS, LANES), jnp.float32),
        ],
    )(lines, turn.astype(jnp.int32).reshape(1, 1), block_diag, block_below, block_above, lines_of)
    improved = swapped(improved, 2)

    def owned_body(*refs):
        owned_kernel(levels, *refs)

    (owned,) = kernel_call(
        owned_body, [f32(sectors, 1, radial)], [VMEM], (devices * radial, devices * radial), "owned"
    )(improved)
    sums = lax.all_to_all(owned, "sec", split_axis=0, concat_axis=0, tiled=True)
    (correction,) = kernel_call(
        finish_kernel, [f32(*tile)], [VMEM], (4 * cell_count, 3 * cell_count), "finish"
    )(improved)
    weak_grad = jnp.sum(sums, axis=0)
    return (correction, weak_grad)


def solution(mesh):
    return jax.shard_map(
        local,
        mesh=mesh,
        in_specs=(
            P("lat", "sec", None),
            P("lat", "sec", None),
            P("lat", "sec", None),
            P("lat", "sec", None),
            P("lat", "sec", None),
            P(),
            P(),
            P(),
            P("sec", "lat", None),
            P("sec", "lat", None, None),
        ),
        out_specs=(P("lat", "sec", None), P("lat", None)),
        check_vma=False,
    )
```

```python
import jax
import jax.numpy as jnp
from jax import lax
from jax.experimental import pallas as pl
from jax.experimental.pallas import tpu as pltpu
from jax.sharding import PartitionSpec as P

LANES = 128
ROWS = 8
WIDTH = LANES // ROWS
FIELDS = 5
FINITE_STEP = 0.03125
YIELD_WEIGHT = 0.25
HIGHEST = lax.Precision.HIGHEST
VMEM = pl.BlockSpec(memory_space=pltpu.VMEM)
HBM = pl.BlockSpec(memory_space=pltpu.HBM)
SMEM = pl.BlockSpec(memory_space=pltpu.SMEM)
MIB = 1024 * 1024


def places():
    row = lax.broadcasted_iota(jnp.int32, (ROWS, LANES), 0)
    lane = lax.broadcasted_iota(jnp.int32, (ROWS, LANES), 1)
    return row, lane // WIDTH, lane % WIDTH


def along_lane(block, row_of):
    return jnp.take_along_axis(block, row_of, axis=0, mode="promise_in_bounds")


def along_row(block, lane_of):
    return jnp.take_along_axis(block, lane_of, axis=1, mode="promise_in_bounds")


def to_lines(block, row_of):
    return along_lane(pltpu.roll(block, 0, 1, stride=WIDTH, stride_axis=0), row_of)


def tile_kernel(
    velocity_far,
    base_far,
    yielded_far,
    colors_far,
    forcing_far,
    lines,
    velocity,
    base,
    yielded,
    colors,
    forcing,
    landed,
):
    arrays = (
        (velocity_far, velocity),
        (base_far, base),
        (yielded_far, yielded),
        (colors_far, colors),
        (forcing_far, forcing),
    )
    copies = [pltpu.make_async_copy(far, near, landed.at[place]) for place, (far, near) in enumerate(arrays)]
    for copy in copies:
        copy.start()
    levels, _, width = velocity.shape
    blocks = width // LANES
    stride = lines.shape[0] // (blocks * ROWS)
    row, group, place = places()
    row_of = (group - row) & (ROWS - 1)
    lane = group * WIDTH + place
    kind = place // ROWS
    low_lane = (group * WIDTH - 1 - kind) & (LANES - 1)
    high_lane = (group * WIDTH + WIDTH + kind) & (LANES - 1)
    x_of = place & (ROWS - 1)
    sides = []
    for copy in copies[:3]:
        copy.wait()
    for level in range(levels):
        v = velocity[level]
        coef = yielded[level].astype(jnp.float32) * YIELD_WEIGHT
        eta = base[level] / (1.0 + coef * v * v)
        outer = []
        for block in range(blocks):
            span = slice(block * LANES, (block + 1) * LANES)
            here = eta[:, span]
            moved = jnp.where(place < ROWS, pltpu.roll(here, 1, 1), pltpu.roll(here, LANES - 1, 1))
            outer.append(jnp.where((place == 0) | (place == WIDTH - 1), v[:, span], moved))
        sides.append(outer)
    for copy in copies[3:]:
        copy.wait()
    for block in range(blocks):
        span = slice(block * LANES, (block + 1) * LANES)
        start = block * ROWS * stride
        rim = jnp.zeros((ROWS, LANES), jnp.float32)
        for level in range(levels):
            low = sides[level][block]
            high = low
            if block > 0:
                low = jnp.where(lane >= LANES - WIDTH, sides[level][block - 1], low)
            else:
                low = jnp.where(lane >= LANES - WIDTH, 0.0, low)
            if block < blocks - 1:
                high = jnp.where(lane < WIDTH, sides[level][block + 1], high)
            else:
                high = jnp.where(lane < WIDTH, 0.0, high)
            for side, picked in enumerate((along_row(low, low_lane), along_row(high, high_lane))):
                rim = jnp.where(row == 2 * level + side, along_lane(picked, x_of), rim)
            sent = (
                velocity[level, :, span],
                base[level, :, span],
                yielded[level, :, span].astype(jnp.float32) * YIELD_WEIGHT,
                FINITE_STEP * (colors[level, :, span] + 1).astype(jnp.float32),
                forcing[level, :, span],
            )
            for field, cells in enumerate(sent):
                lines[pl.ds(start + field * levels + level, ROWS, stride=stride), :] = to_lines(cells, row_of)
        rim = to_lines(rim, row_of)
        for spare in range(FIELDS * levels, stride):
            lines[pl.ds(start + spare, ROWS, stride=stride), :] = rim


def spread_rows(received, stride, field, levels, store):
    blocks = received.shape[0] // (stride * ROWS)
    for level in range(levels):
        for block in range(blocks):
            rows = received[pl.ds(block * ROWS * stride + field * levels + level, ROWS, stride=stride), :]
            store(block * ROWS * levels + level, rows)


def edge_kernel(levels, received, turn, velocity, viscosity, base, coef, low_edge, high_edge):
    radial = base.shape[0]
    stride = received.shape[0] * levels // radial
    nothing = jnp.zeros((ROWS, LANES), jnp.float32)
    for padded in (velocity, viscosity):
        padded[pl.ds(0, ROWS), :] = nothing
        padded[pl.ds(radial + ROWS, ROWS), :] = nothing

    def store_velocity(first, rows):
        velocity[pl.ds(ROWS + first, ROWS, stride=levels), :] = rows

    def store_base(first, rows):
        base[pl.ds(first, ROWS, stride=levels), :] = rows

    def store_coef(first, rows):
        coef[pl.ds(first, ROWS, stride=levels), :] = rows

    for field, store in enumerate((store_velocity, store_base, store_coef)):
        spread_rows(received, stride, field, levels, store)
    _, group, place = places()
    shift = turn[0, 0]
    first_lane = shift * WIDTH + place
    last_lane = ((shift + ROWS - 1) & (ROWS - 1)) * WIDTH + place
    for start in range(0, radial, ROWS):
        v = velocity[pl.ds(ROWS + start, ROWS), :]
        eta = base[pl.ds(start, ROWS), :] / (1.0 + coef[pl.ds(start, ROWS), :] * v * v)
        viscosity[pl.ds(ROWS + start, ROWS), :] = eta
        for kind, cells in enumerate((v, eta)):
            for edge, lane_of in ((low_edge, first_lane), (high_edge, last_lane)):
                edge[kind, pl.ds(start // ROWS, 1), :] = along_lane(along_row(cells, lane_of), group)[:1]


def middle_kernel(levels, received, turn, velocity, viscosity, base, coef, out, step, forcing):
    radial = base.shape[0]
    stride = received.shape[0] * levels // radial

    def store_step(first, rows):
        step[pl.ds(first, ROWS, stride=levels), :] = rows

    def store_forcing(first, rows):
        forcing[pl.ds(first, ROWS, stride=levels), :] = rows

    spread_rows(received, stride, 3, levels, store_step)
    spread_rows(received, stride, 4, levels, store_forcing)
    row, group, place = places()
    shift = turn[0, 0]
    x = (group - shift) & (ROWS - 1)
    first_x, last_x = x == 0, x == ROWS - 1
    first_y, last_y = place == 0, place == WIDTH - 1
    slot = 2 * (row % levels) + jnp.where(first_y, 0, 1)
    v_lane = ((slot + shift) & (ROWS - 1)) * WIDTH + x
    eta_lane = v_lane + ROWS

    def lateral(block, y_rim):
        return (
            jnp.where(first_x, 0.0, pltpu.roll(block, WIDTH, 1)),
            jnp.where(last_x, 0.0, pltpu.roll(block, LANES - WIDTH, 1)),
            jnp.where(first_y, y_rim, pltpu.roll(block, 1, 1)),
            jnp.where(last_y, y_rim, pltpu.roll(block, LANES - 1, 1)),
        )

    for start in range(0, radial, ROWS):
        here = pl.ds(start, ROWS)
        v = velocity[pl.ds(ROWS + start, ROWS), :]
        v_low = velocity[pl.ds(ROWS + start - 1, ROWS), :]
        v_high = velocity[pl.ds(ROWS + start + 1, ROWS), :]
        eta = viscosity[pl.ds(ROWS + start, ROWS), :]
        eta_low = viscosity[pl.ds(ROWS + start - 1, ROWS), :]
        eta_high = viscosity[pl.ds(ROWS + start + 1, ROWS), :]
        b = base[here, :]
        amount = coef[here, :]
        source = start // levels * stride + FIELDS * levels
        rim = received[pl.ds(source, 1), :]
        for later in range(1, ROWS // levels):
            rim = jnp.where(row < later * levels, rim, received[pl.ds(source + later * stride, 1), :])
        near_v = lateral(v, along_row(rim, v_lane)) + (v_low, v_high)
        near_eta = lateral(eta, along_row(rim, eta_lane)) + (eta_low, eta_high)
        value_sum = near_v[0]
        eta_sum = near_eta[0]
        product_sum = near_v[0] * near_eta[0]
        for near_value, near_visc in zip(near_v[1:], near_eta[1:]):
            value_sum = value_sum + near_value
            eta_sum = eta_sum + near_visc
            product_sum = product_sum + near_value * near_visc
        moved = v + step[here, :]
        moved_inverse = 1.0 / (1.0 + amount * moved * moved)
        moved_eta = b * moved_inverse
        slope = -amount * (moved + v) * eta * moved_inverse
        out[0, here, :] = value_sum
        out[1, here, :] = eta_sum
        out[2, here, :] = product_sum
        out[3, here, :] = slope
        out[4, here, :] = b * v - forcing[here, :]
        out[5, here, :] = 3.0 * moved_eta + b
        out[6, here, :] = 0.5 * (slope * (v_low - v) - eta_low - moved_eta)
        out[7, here, :] = 0.5 * (slope * (v_high - v) - eta_high - moved_eta)


def lines_kernel(line_ids, owner_ids, lines_of):
    entries = line_ids.shape[1]
    owner_count, line_count = lines_of.shape
    picks = (lax.broadcasted_iota(jnp.int32, (line_count, entries), 0) == line_ids[...]).astype(jnp.float32)
    owners = (lax.broadcasted_iota(jnp.int32, (owner_count, entries), 0) == owner_ids[...]).astype(jnp.float32)
    lines_of[...] = lax.dot_general(
        owners, picks, (((1,), (1,)), ((), ())), preferred_element_type=jnp.float32
    )


def pencil_kernel(
    levels,
    velocity,
    viscosity,
    middle,
    left,
    right,
    turn,
    block_diag,
    block_below,
    block_above,
    lines_of,
    out,
    work,
):
    radial = work.shape[1]
    devices = radial // levels
    row, group, place = places()
    x = (group - turn[0, 0]) & (ROWS - 1)
    first_x, last_x = x == 0, x == ROWS - 1
    own_lane = row * WIDTH + place

    def side(kind, start):
        low = along_row(jnp.broadcast_to(left[kind, pl.ds(start // ROWS, 1), :], (ROWS, LANES)), own_lane)
        high = along_row(jnp.broadcast_to(right[kind, pl.ds(start // ROWS, 1), :], (ROWS, LANES)), own_lane)
        return jnp.where(first_x, low, jnp.where(last_x, high, 0.0))

    for start in range(0, radial, ROWS):
        here = pl.ds(start, ROWS)
        v = velocity[pl.ds(ROWS + start, ROWS), :]
        eta = viscosity[pl.ds(ROWS + start, ROWS), :]
        v_rim = side(0, start)
        eta_rim = side(1, start)
        value_sum = middle[0, here, :] + v_rim
        eta_sum = middle[1, here, :] + eta_rim
        product_sum = middle[2, here, :] + v_rim * eta_rim
        spread = 6.0 * v - value_sum
        sensitivity = 0.5 * eta * spread
        work[0, here, :] = sensitivity + 0.5 * (v * eta_sum - product_sum) + middle[4, here, :]
        work[1, here, :] = 0.5 * eta_sum + 0.5 * middle[3, here, :] * spread + middle[5, here, :]
        work[2, here, :] = sensitivity

    residual = work[0]
    half = radial // 2

    def apply_blocks(field):
        head, tail = field[:half], field[half:]
        first = jnp.dot(block_diag[0], head, precision=HIGHEST, preferred_element_type=jnp.float32)
        first = first + jnp.dot(block_above[0], tail, precision=HIGHEST, preferred_element_type=jnp.float32)
        second = jnp.dot(block_diag[1], tail, precision=HIGHEST, preferred_element_type=jnp.float32)
        second = second + jnp.dot(block_below[1], head, precision=HIGHEST, preferred_element_type=jnp.float32)
        return jnp.concatenate([first, second], axis=0)

    initial = apply_blocks(residual)
    level_index = lax.broadcasted_iota(jnp.int32, (radial, LANES), 0)
    from_above = jnp.where(level_index == radial - 1, 0.0, pltpu.roll(middle[6] * initial, radial - 1, 0))
    from_below = jnp.where(level_index == 0, 0.0, pltpu.roll(middle[7] * initial, 1, 0))
    remainder = residual - (work[1] * initial + from_above + from_below)
    correction = initial + apply_blocks(remainder)
    gradient = correction * work[2]
    owned = lax.dot_general(
        lines_of[...],
        gradient,
        (((1,), (1,)), ((), ())),
        precision=HIGHEST,
        preferred_element_type=jnp.float32,
    )
    work[0] = correction
    parts = radial // LANES
    back = levels + parts
    for block in range(devices // ROWS):
        for level in range(levels):
            out[pl.ds(block * ROWS * back + level, ROWS, stride=back), :] = work[
                0, pl.ds(block * ROWS * levels + level, ROWS, stride=levels), :
            ]
        for part in range(parts):
            out[pl.ds(block * ROWS * back + levels + part, ROWS, stride=back), :] = owned[
                block * ROWS : (block + 1) * ROWS, part * LANES : (part + 1) * LANES
            ]


def owned_kernel(levels, received, owned):
    sectors, _, radial = owned.shape
    parts = radial // LANES
    back = levels + parts
    blocks = received.shape[0] // (back * ROWS)
    for part in range(parts):
        total = received[pl.ds(levels + part, ROWS, stride=back), :]
        for block in range(1, blocks):
            total = total + received[pl.ds(block * ROWS * back + levels + part, ROWS, stride=back), :]
        total = jnp.sum(total, axis=0, keepdims=True)
        for sector in range(sectors):
            owned[sector, :, part * LANES : (part + 1) * LANES] = total


def finish_kernel(received, correction):
    levels, rows, width = correction.shape
    blocks = width // LANES
    back = received.shape[0] // (blocks * ROWS)
    row, group, place = places()
    row_of = (group - row) & (ROWS - 1)
    lane_of = ((group + row) & (ROWS - 1)) * WIDTH + place
    for level in range(levels):
        for block in range(blocks):
            lines = received[pl.ds(block * ROWS * back + level, ROWS, stride=back), :]
            correction[level, :, block * LANES : (block + 1) * LANES] = along_row(
                along_lane(lines, row_of), lane_of
            )


def shifted(cells, axis, step):
    count = lax.axis_size(axis)
    return lax.ppermute(cells, axis, [(i, i + step) for i in range(count) if 0 <= i + step < count])


def swapped(rows, parts):
    devices = lax.axis_size("lat")
    sent = rows.reshape(devices, -1, parts, LANES)
    taken = lax.all_to_all(sent, "lat", split_axis=0, concat_axis=0, tiled=True)
    return taken.reshape(rows.shape)


def kernel_call(body, shapes, specs, work, name, scratch=()):
    return pl.pallas_call(
        body,
        out_shape=shapes,
        in_specs=specs,
        out_specs=[VMEM] * len(shapes),
        scratch_shapes=scratch,
        compiler_params=pltpu.CompilerParams(vmem_limit_bytes=32 * MIB),
        cost_estimate=pl.CostEstimate(flops=work[0], bytes_accessed=4 * work[1], transcendentals=0),
        name=name,
    )


def f32(*shape):
    return jax.ShapeDtypeStruct(shape, jnp.float32)


def local(
    velocity,
    base_visc,
    yielded,
    colors,
    forcing,
    block_diag,
    block_below,
    block_above,
    weak_lines,
    weak_owner,
):
    levels, rows, width = velocity.shape
    devices = lax.axis_size("lat")
    sectors = lax.axis_size("sec")
    radial = levels * devices
    cell_count = levels * rows * width
    tile = (levels, rows, width)
    sent_rows = FIELDS * levels + 2
    far = [
        pltpu.with_memory_space_constraint(array, pltpu.HBM)
        for array in (velocity, base_visc, yielded, colors, forcing)
    ]
    (lines,) = kernel_call(
        tile_kernel,
        [f32(devices * sent_rows, LANES)],
        [HBM] * FIELDS,
        (40 * cell_count, 12 * cell_count),
        "tile",
        [pltpu.VMEM(tile, array.dtype) for array in far]
        + [pltpu.SemaphoreType.DMA((FIELDS,))],
    )(*far)
    lines = swapped(lines, 2)

    picked = weak_lines.reshape(1, -1)
    turn = lax.axis_index("lat") & (rows - 1)
    place = (turn + picked // WIDTH) & (rows - 1)
    line_ids = place * WIDTH + picked % WIDTH
    (lines_of,) = kernel_call(
        lines_kernel,
        [f32(devices, LANES)],
        [VMEM] * 2,
        (2 * devices * LANES * 64, devices * LANES),
        "lines",
    )(line_ids, weak_owner.reshape(1, -1))
    back = levels + radial // LANES
    turn = turn.astype(jnp.int32).reshape(1, 1)
    padded = f32(radial + 2 * ROWS, LANES)
    whole = f32(radial, LANES)
    edge = f32(2, radial // ROWS, LANES)

    def edge_body(*refs):
        edge_kernel(levels, *refs)

    def middle_body(*refs):
        middle_kernel(levels, *refs)

    def pencil_body(*refs):
        pencil_kernel(levels, *refs)

    v, eta, base, coef, low_edge, high_edge = kernel_call(
        edge_body,
        [padded, padded, whole, whole, edge, edge],
        [VMEM, SMEM],
        (10 * cell_count, 7 * cell_count),
        "edges",
    )(lines, turn)
    left = shifted(high_edge, "sec", 1)
    right = shifted(low_edge, "sec", -1)
    (middle,) = kernel_call(
        middle_body,
        [f32(8, radial, LANES)],
        [VMEM, SMEM] + [VMEM] * 4,
        (60 * cell_count, 14 * cell_count),
        "middle",
        [pltpu.VMEM((radial, LANES), jnp.float32), pltpu.VMEM((radial, LANES), jnp.float32)],
    )(lines, turn, v, eta, base, coef)
    (improved,) = kernel_call(
        pencil_body,
        [f32(devices * back, LANES)],
        [VMEM] * 5 + [SMEM] + [VMEM] * 4,
        (24 * radial * radial * LANES, 12 * radial * LANES),
        "pencil",
        [pltpu.VMEM((3, radial, LANES), jnp.float32)],
    )(v, eta, middle, left, right, turn, block_diag, block_below, block_above, lines_of)
    improved = swapped(improved, 2)

    def owned_body(*refs):
        owned_kernel(levels, *refs)

    (owned,) = kernel_call(
        owned_body, [f32(sectors, 1, radial)], [VMEM], (devices * radial, devices * radial), "owned"
    )(improved)
    sums = lax.all_to_all(owned, "sec", split_axis=0, concat_axis=0, tiled=True)
    (correction,) = kernel_call(
        finish_kernel, [f32(*tile)], [VMEM], (4 * cell_count, 3 * cell_count), "finish"
    )(improved)
    weak_grad = jnp.sum(sums, axis=0)
    return (correction, weak_grad)


def solution(mesh):
    return jax.shard_map(
        local,
        mesh=mesh,
        in_specs=(
            P("lat", "sec", None),
            P("lat", "sec", None),
            P("lat", "sec", None),
            P("lat", "sec", None),
            P("lat", "sec", None),
            P(),
            P(),
            P(),
            P("sec", "lat", None),
            P("sec", "lat", None, None),
        ),
        out_specs=(P("lat", "sec", None), P("lat", None)),
        check_vma=False,
    )
```

```python
import jax
import jax.numpy as jnp
from jax import lax
from jax.experimental import pallas as pl
from jax.experimental.pallas import tpu as pltpu
from jax.sharding import PartitionSpec as P

LANES = 128
ROWS = 8
WIDTH = LANES // ROWS
FIELDS = 5
FINITE_STEP = 0.03125
YIELD_WEIGHT = 0.25
HIGHEST = lax.Precision.HIGHEST
VMEM = pl.BlockSpec(memory_space=pltpu.VMEM)
HBM = pl.BlockSpec(memory_space=pltpu.HBM)
SMEM = pl.BlockSpec(memory_space=pltpu.SMEM)
MIB = 1024 * 1024


def places():
    row = lax.broadcasted_iota(jnp.int32, (ROWS, LANES), 0)
    lane = lax.broadcasted_iota(jnp.int32, (ROWS, LANES), 1)
    return row, lane // WIDTH, lane % WIDTH


def along_lane(block, row_of):
    return jnp.take_along_axis(block, row_of, axis=0, mode="promise_in_bounds")


def along_row(block, lane_of):
    return jnp.take_along_axis(block, lane_of, axis=1, mode="promise_in_bounds")


def to_lines(block, row_of):
    return along_lane(pltpu.roll(block, 0, 1, stride=WIDTH, stride_axis=0), row_of)


def tile_kernel(
    velocity_far,
    base_far,
    yielded_far,
    colors_far,
    forcing_far,
    lines_far,
    lines,
    velocity,
    base,
    yielded,
    colors,
    forcing,
    landed,
    left,
):
    arrays = (
        (velocity_far, velocity),
        (base_far, base),
        (yielded_far, yielded),
        (colors_far, colors),
        (forcing_far, forcing),
    )
    copies = [pltpu.make_async_copy(far, near, landed.at[place]) for place, (far, near) in enumerate(arrays)]
    for copy in copies:
        copy.start()
    levels, _, width = velocity.shape
    blocks = width // LANES
    stride = lines.shape[0] // (blocks * ROWS)
    row, group, place = places()
    row_of = (group - row) & (ROWS - 1)
    lane = group * WIDTH + place
    kind = place // ROWS
    low_lane = (group * WIDTH - 1 - kind) & (LANES - 1)
    high_lane = (group * WIDTH + WIDTH + kind) & (LANES - 1)
    x_of = place & (ROWS - 1)
    sides = []
    for copy in copies[:3]:
        copy.wait()
    for level in range(levels):
        v = velocity[level]
        coef = yielded[level].astype(jnp.float32) * YIELD_WEIGHT
        eta = base[level] / (1.0 + coef * v * v)
        outer = []
        for block in range(blocks):
            span = slice(block * LANES, (block + 1) * LANES)
            here = eta[:, span]
            moved = jnp.where(place < ROWS, pltpu.roll(here, 1, 1), pltpu.roll(here, LANES - 1, 1))
            outer.append(jnp.where((place == 0) | (place == WIDTH - 1), v[:, span], moved))
        sides.append(outer)
    for copy in copies[3:]:
        copy.wait()
    writes = []
    for block in range(blocks):
        span = slice(block * LANES, (block + 1) * LANES)
        start = block * ROWS * stride
        rim = jnp.zeros((ROWS, LANES), jnp.float32)
        for level in range(levels):
            low = sides[level][block]
            high = low
            if block > 0:
                low = jnp.where(lane >= LANES - WIDTH, sides[level][block - 1], low)
            else:
                low = jnp.where(lane >= LANES - WIDTH, 0.0, low)
            if block < blocks - 1:
                high = jnp.where(lane < WIDTH, sides[level][block + 1], high)
            else:
                high = jnp.where(lane < WIDTH, 0.0, high)
            for side, picked in enumerate((along_row(low, low_lane), along_row(high, high_lane))):
                rim = jnp.where(row == 2 * level + side, along_lane(picked, x_of), rim)
            sent = (
                velocity[level, :, span],
                base[level, :, span],
                yielded[level, :, span].astype(jnp.float32) * YIELD_WEIGHT,
                FINITE_STEP * (colors[level, :, span] + 1).astype(jnp.float32),
                forcing[level, :, span],
            )
            for field, cells in enumerate(sent):
                lines[pl.ds(start + field * levels + level, ROWS, stride=stride), :] = to_lines(cells, row_of)
        rim = to_lines(rim, row_of)
        lines[pl.ds(start + FIELDS * levels, ROWS, stride=stride), :] = rim
        part = pl.ds(start, ROWS * stride)
        copy = pltpu.make_async_copy(lines.at[part], lines_far.at[part], left.at[block])
        copy.start()
        writes.append(copy)
    for copy in writes:
        copy.wait()


def spread_rows(received, stride, field, levels, store):
    blocks = received.shape[0] // (stride * ROWS)
    for level in range(levels):
        for block in range(blocks):
            rows = received[pl.ds(block * ROWS * stride + field * levels + level, ROWS, stride=stride), :]
            store(block * ROWS * levels + level, rows)


def edge_kernel(levels, received, turn, velocity, viscosity, base, coef, low_edge, high_edge):
    radial = base.shape[0]
    stride = received.shape[0] * levels // radial
    nothing = jnp.zeros((ROWS, LANES), jnp.float32)
    for padded in (velocity, viscosity):
        padded[pl.ds(0, ROWS), :] = nothing
        padded[pl.ds(radial + ROWS, ROWS), :] = nothing

    def store_velocity(first, rows):
        velocity[pl.ds(ROWS + first, ROWS, stride=levels), :] = rows

    def store_base(first, rows):
        base[pl.ds(first, ROWS, stride=levels), :] = rows

    def store_coef(first, rows):
        coef[pl.ds(first, ROWS, stride=levels), :] = rows

    for field, store in enumerate((store_velocity, store_base, store_coef)):
        spread_rows(received, stride, field, levels, store)
    _, group, place = places()
    shift = turn[0, 0]
    first_lane = shift * WIDTH + place
    last_lane = ((shift + ROWS - 1) & (ROWS - 1)) * WIDTH + place
    for start in range(0, radial, ROWS):
        v = velocity[pl.ds(ROWS + start, ROWS), :]
        eta = base[pl.ds(start, ROWS), :] / (1.0 + coef[pl.ds(start, ROWS), :] * v * v)
        viscosity[pl.ds(ROWS + start, ROWS), :] = eta
        for kind, cells in enumerate((v, eta)):
            for edge, lane_of in ((low_edge, first_lane), (high_edge, last_lane)):
                edge[kind, pl.ds(start // ROWS, 1), :] = along_lane(along_row(cells, lane_of), group)[:1]


def middle_kernel(levels, received, turn, velocity, viscosity, base, coef, out, step, forcing):
    radial = base.shape[0]
    stride = received.shape[0] * levels // radial

    def store_step(first, rows):
        step[pl.ds(first, ROWS, stride=levels), :] = rows

    def store_forcing(first, rows):
        forcing[pl.ds(first, ROWS, stride=levels), :] = rows

    spread_rows(received, stride, 3, levels, store_step)
    spread_rows(received, stride, 4, levels, store_forcing)
    row, group, place = places()
    shift = turn[0, 0]
    x = (group - shift) & (ROWS - 1)
    first_x, last_x = x == 0, x == ROWS - 1
    first_y, last_y = place == 0, place == WIDTH - 1
    slot = 2 * (row % levels) + jnp.where(first_y, 0, 1)
    v_lane = ((slot + shift) & (ROWS - 1)) * WIDTH + x
    eta_lane = v_lane + ROWS

    def lateral(block, y_rim):
        return (
            jnp.where(first_x, 0.0, pltpu.roll(block, WIDTH, 1)),
            jnp.where(last_x, 0.0, pltpu.roll(block, LANES - WIDTH, 1)),
            jnp.where(first_y, y_rim, pltpu.roll(block, 1, 1)),
            jnp.where(last_y, y_rim, pltpu.roll(block, LANES - 1, 1)),
        )

    for start in range(0, radial, ROWS):
        here = pl.ds(start, ROWS)
        v = velocity[pl.ds(ROWS + start, ROWS), :]
        v_low = velocity[pl.ds(ROWS + start - 1, ROWS), :]
        v_high = velocity[pl.ds(ROWS + start + 1, ROWS), :]
        eta = viscosity[pl.ds(ROWS + start, ROWS), :]
        eta_low = viscosity[pl.ds(ROWS + start - 1, ROWS), :]
        eta_high = viscosity[pl.ds(ROWS + start + 1, ROWS), :]
        b = base[here, :]
        amount = coef[here, :]
        source = start // levels * stride + FIELDS * levels
        rim = received[pl.ds(source, 1), :]
        for later in range(1, ROWS // levels):
            rim = jnp.where(row < later * levels, rim, received[pl.ds(source + later * stride, 1), :])
        near_v = lateral(v, along_row(rim, v_lane)) + (v_low, v_high)
        near_eta = lateral(eta, along_row(rim, eta_lane)) + (eta_low, eta_high)
        value_sum = near_v[0]
        eta_sum = near_eta[0]
        product_sum = near_v[0] * near_eta[0]
        for near_value, near_visc in zip(near_v[1:], near_eta[1:]):
            value_sum = value_sum + near_value
            eta_sum = eta_sum + near_visc
            product_sum = product_sum + near_value * near_visc
        moved = v + step[here, :]
        moved_inverse = 1.0 / (1.0 + amount * moved * moved)
        moved_eta = b * moved_inverse
        slope = -amount * (moved + v) * eta * moved_inverse
        out[0, here, :] = value_sum
        out[1, here, :] = eta_sum
        out[2, here, :] = product_sum
        out[3, here, :] = slope
        out[4, here, :] = b * v - forcing[here, :]
        out[5, here, :] = 3.0 * moved_eta + b
        out[6, here, :] = 0.5 * (slope * (v_low - v) - eta_low - moved_eta)
        out[7, here, :] = 0.5 * (slope * (v_high - v) - eta_high - moved_eta)


def lines_kernel(line_ids, owner_ids, lines_of):
    entries = line_ids.shape[1]
    owner_count, line_count = lines_of.shape
    picks = (lax.broadcasted_iota(jnp.int32, (line_count, entries), 0) == line_ids[...]).astype(jnp.float32)
    owners = (lax.broadcasted_iota(jnp.int32, (owner_count, entries), 0) == owner_ids[...]).astype(jnp.float32)
    lines_of[...] = lax.dot_general(
        owners, picks, (((1,), (1,)), ((), ())), preferred_element_type=jnp.float32
    )


def pencil_kernel(
    levels,
    velocity,
    viscosity,
    middle,
    left,
    right,
    turn,
    block_diag,
    block_below,
    block_above,
    lines_of,
    out,
    work,
):
    radial = work.shape[1]
    devices = radial // levels
    row, group, place = places()
    x = (group - turn[0, 0]) & (ROWS - 1)
    first_x, last_x = x == 0, x == ROWS - 1
    own_lane = row * WIDTH + place

    def side(kind, start):
        low = along_row(jnp.broadcast_to(left[kind, pl.ds(start // ROWS, 1), :], (ROWS, LANES)), own_lane)
        high = along_row(jnp.broadcast_to(right[kind, pl.ds(start // ROWS, 1), :], (ROWS, LANES)), own_lane)
        return jnp.where(first_x, low, jnp.where(last_x, high, 0.0))

    for start in range(0, radial, ROWS):
        here = pl.ds(start, ROWS)
        v = velocity[pl.ds(ROWS + start, ROWS), :]
        eta = viscosity[pl.ds(ROWS + start, ROWS), :]
        v_rim = side(0, start)
        eta_rim = side(1, start)
        value_sum = middle[0, here, :] + v_rim
        eta_sum = middle[1, here, :] + eta_rim
        product_sum = middle[2, here, :] + v_rim * eta_rim
        spread = 6.0 * v - value_sum
        sensitivity = 0.5 * eta * spread
        work[0, here, :] = sensitivity + 0.5 * (v * eta_sum - product_sum) + middle[4, here, :]
        work[1, here, :] = 0.5 * eta_sum + 0.5 * middle[3, here, :] * spread + middle[5, here, :]
        work[2, here, :] = sensitivity

    residual = work[0]
    half = radial // 2

    def apply_blocks(field):
        head, tail = field[:half], field[half:]
        first = jnp.dot(block_diag[0], head, precision=HIGHEST, preferred_element_type=jnp.float32)
        first = first + jnp.dot(block_above[0], tail, precision=HIGHEST, preferred_element_type=jnp.float32)
        second = jnp.dot(block_diag[1], tail, precision=HIGHEST, preferred_element_type=jnp.float32)
        second = second + jnp.dot(block_below[1], head, precision=HIGHEST, preferred_element_type=jnp.float32)
        return jnp.concatenate([first, second], axis=0)

    initial = apply_blocks(residual)
    level_index = lax.broadcasted_iota(jnp.int32, (radial, LANES), 0)
    from_above = jnp.where(level_index == radial - 1, 0.0, pltpu.roll(middle[6] * initial, radial - 1, 0))
    from_below = jnp.where(level_index == 0, 0.0, pltpu.roll(middle[7] * initial, 1, 0))
    remainder = residual - (work[1] * initial + from_above + from_below)
    correction = initial + apply_blocks(remainder)
    gradient = correction * work[2]
    owned = lax.dot_general(
        lines_of[...],
        gradient,
        (((1,), (1,)), ((), ())),
        precision=HIGHEST,
        preferred_element_type=jnp.float32,
    )
    work[0] = correction
    parts = radial // LANES
    back = levels + parts
    for block in range(devices // ROWS):
        for level in range(levels):
            out[pl.ds(block * ROWS * back + level, ROWS, stride=back), :] = work[
                0, pl.ds(block * ROWS * levels + level, ROWS, stride=levels), :
            ]
        for part in range(parts):
            out[pl.ds(block * ROWS * back + levels + part, ROWS, stride=back), :] = owned[
                block * ROWS : (block + 1) * ROWS, part * LANES : (part + 1) * LANES
            ]


def owned_kernel(levels, received, owned):
    sectors, _, radial = owned.shape
    parts = radial // LANES
    back = levels + parts
    blocks = received.shape[0] // (back * ROWS)
    for part in range(parts):
        total = received[pl.ds(levels + part, ROWS, stride=back), :]
        for block in range(1, blocks):
            total = total + received[pl.ds(block * ROWS * back + levels + part, ROWS, stride=back), :]
        total = jnp.sum(total, axis=0, keepdims=True)
        for sector in range(sectors):
            owned[sector, :, part * LANES : (part + 1) * LANES] = total


def finish_kernel(received, correction):
    levels, rows, width = correction.shape
    blocks = width // LANES
    back = received.shape[0] // (blocks * ROWS)
    row, group, place = places()
    row_of = (group - row) & (ROWS - 1)
    lane_of = ((group + row) & (ROWS - 1)) * WIDTH + place
    for level in range(levels):
        for block in range(blocks):
            lines = received[pl.ds(block * ROWS * back + level, ROWS, stride=back), :]
            correction[level, :, block * LANES : (block + 1) * LANES] = along_row(
                along_lane(lines, row_of), lane_of
            )


def shifted(cells, axis, step):
    count = lax.axis_size(axis)
    return lax.ppermute(cells, axis, [(i, i + step) for i in range(count) if 0 <= i + step < count])


def swapped(rows, parts):
    devices = lax.axis_size("lat")
    sent = rows.reshape(devices, -1, parts, LANES)
    taken = lax.all_to_all(sent, "lat", split_axis=0, concat_axis=0, tiled=True)
    return taken.reshape(rows.shape)


def kernel_call(body, shapes, specs, work, name, scratch=(), into=VMEM):
    return pl.pallas_call(
        body,
        out_shape=shapes,
        in_specs=specs,
        out_specs=[into] * len(shapes),
        scratch_shapes=scratch,
        compiler_params=pltpu.CompilerParams(vmem_limit_bytes=32 * MIB),
        cost_estimate=pl.CostEstimate(flops=work[0], bytes_accessed=4 * work[1], transcendentals=0),
        name=name,
    )


def f32(*shape):
    return jax.ShapeDtypeStruct(shape, jnp.float32)


def local(
    velocity,
    base_visc,
    yielded,
    colors,
    forcing,
    block_diag,
    block_below,
    block_above,
    weak_lines,
    weak_owner,
):
    levels, rows, width = velocity.shape
    devices = lax.axis_size("lat")
    sectors = lax.axis_size("sec")
    radial = levels * devices
    cell_count = levels * rows * width
    tile = (levels, rows, width)
    sent_rows = FIELDS * levels + 1
    far = [
        pltpu.with_memory_space_constraint(array, pltpu.HBM)
        for array in (velocity, base_visc, yielded, colors, forcing)
    ]
    (lines,) = kernel_call(
        tile_kernel,
        [f32(devices * sent_rows, LANES)],
        [HBM] * FIELDS,
        (40 * cell_count, 12 * cell_count),
        "tile",
        [pltpu.VMEM((devices * sent_rows, LANES), jnp.float32)]
        + [pltpu.VMEM(tile, array.dtype) for array in far]
        + [pltpu.SemaphoreType.DMA((FIELDS,)), pltpu.SemaphoreType.DMA((width // LANES,))],
        HBM,
    )(*far)
    lines = swapped(lines, 1)

    picked = weak_lines.reshape(1, -1)
    turn = lax.axis_index("lat") & (rows - 1)
    place = (turn + picked // WIDTH) & (rows - 1)
    line_ids = place * WIDTH + picked % WIDTH
    (lines_of,) = kernel_call(
        lines_kernel,
        [f32(devices, LANES)],
        [VMEM] * 2,
        (2 * devices * LANES * 64, devices * LANES),
        "lines",
    )(line_ids, weak_owner.reshape(1, -1))
    back = levels + radial // LANES
    turn = turn.astype(jnp.int32).reshape(1, 1)
    padded = f32(radial + 2 * ROWS, LANES)
    whole = f32(radial, LANES)
    edge = f32(2, radial // ROWS, LANES)

    def edge_body(*refs):
        edge_kernel(levels, *refs)

    def middle_body(*refs):
        middle_kernel(levels, *refs)

    def pencil_body(*refs):
        pencil_kernel(levels, *refs)

    v, eta, base, coef, low_edge, high_edge = kernel_call(
        edge_body,
        [padded, padded, whole, whole, edge, edge],
        [VMEM, SMEM],
        (10 * cell_count, 7 * cell_count),
        "edges",
    )(lines, turn)
    left = shifted(high_edge, "sec", 1)
    right = shifted(low_edge, "sec", -1)
    (middle,) = kernel_call(
        middle_body,
        [f32(8, radial, LANES)],
        [VMEM, SMEM] + [VMEM] * 4,
        (60 * cell_count, 14 * cell_count),
        "middle",
        [pltpu.VMEM((radial, LANES), jnp.float32), pltpu.VMEM((radial, LANES), jnp.float32)],
    )(lines, turn, v, eta, base, coef)
    (improved,) = kernel_call(
        pencil_body,
        [f32(devices * back, LANES)],
        [VMEM] * 5 + [SMEM] + [VMEM] * 4,
        (24 * radial * radial * LANES, 12 * radial * LANES),
        "pencil",
        [pltpu.VMEM((3, radial, LANES), jnp.float32)],
    )(v, eta, middle, left, right, turn, block_diag, block_below, block_above, lines_of)
    improved = swapped(improved, 2)

    def owned_body(*refs):
        owned_kernel(levels, *refs)

    (owned,) = kernel_call(
        owned_body, [f32(sectors, 1, radial)], [VMEM], (devices * radial, devices * radial), "owned"
    )(improved)
    sums = lax.all_to_all(owned, "sec", split_axis=0, concat_axis=0, tiled=True)
    (correction,) = kernel_call(
        finish_kernel, [f32(*tile)], [VMEM], (4 * cell_count, 3 * cell_count), "finish"
    )(improved)
    weak_grad = jnp.sum(sums, axis=0)
    return (correction, weak_grad)


def solution(mesh):
    return jax.shard_map(
        local,
        mesh=mesh,
        in_specs=(
            P("lat", "sec", None),
            P("lat", "sec", None),
            P("lat", "sec", None),
            P("lat", "sec", None),
            P("lat", "sec", None),
            P(),
            P(),
            P(),
            P("sec", "lat", None),
            P("sec", "lat", None, None),
        ),
        out_specs=(P("lat", "sec", None), P("lat", None)),
        check_vma=False,
    )
```

```python
import jax
import jax.numpy as jnp
from jax import lax
from jax.experimental import pallas as pl
from jax.experimental.pallas import tpu as pltpu
from jax.sharding import PartitionSpec as P

LANES = 128
ROWS = 8
WIDTH = LANES // ROWS
FIELDS = 5
FINITE_STEP = 0.03125
YIELD_WEIGHT = 0.25
HIGHEST = lax.Precision.HIGHEST
VMEM = pl.BlockSpec(memory_space=pltpu.VMEM)
HBM = pl.BlockSpec(memory_space=pltpu.HBM)
MIB = 1024 * 1024


def places():
    row = lax.broadcasted_iota(jnp.int32, (ROWS, LANES), 0)
    lane = lax.broadcasted_iota(jnp.int32, (ROWS, LANES), 1)
    return row, lane // WIDTH, lane % WIDTH


def along_lane(block, row_of):
    return jnp.take_along_axis(block, row_of, axis=0, mode="promise_in_bounds")


def along_row(block, lane_of):
    return jnp.take_along_axis(block, lane_of, axis=1, mode="promise_in_bounds")


def to_lines(block, row_of):
    return along_lane(pltpu.roll(block, 0, 1, stride=WIDTH, stride_axis=0), row_of)


def tile_kernel(
    velocity_far,
    base_far,
    yielded_far,
    colors_far,
    forcing_far,
    lines,
    velocity,
    base,
    yielded,
    colors,
    forcing,
    landed,
):
    arrays = (
        (velocity_far, velocity),
        (base_far, base),
        (yielded_far, yielded),
        (colors_far, colors),
        (forcing_far, forcing),
    )
    copies = [pltpu.make_async_copy(far, near, landed.at[place]) for place, (far, near) in enumerate(arrays)]
    for copy in copies:
        copy.start()
    levels, _, width = velocity.shape
    blocks = width // LANES
    stride = lines.shape[0] // (blocks * ROWS)
    row, group, place = places()
    row_of = (group - row) & (ROWS - 1)
    lane = group * WIDTH + place
    kind = place // ROWS
    low_lane = (group * WIDTH - 1 - kind) & (LANES - 1)
    high_lane = (group * WIDTH + WIDTH + kind) & (LANES - 1)
    x_of = place & (ROWS - 1)
    sides = []
    for copy in copies[:3]:
        copy.wait()
    for level in range(levels):
        v = velocity[level]
        coef = yielded[level].astype(jnp.float32) * YIELD_WEIGHT
        eta = base[level] / (1.0 + coef * v * v)
        outer = []
        for block in range(blocks):
            span = slice(block * LANES, (block + 1) * LANES)
            here = eta[:, span]
            moved = jnp.where(place < ROWS, pltpu.roll(here, 1, 1), pltpu.roll(here, LANES - 1, 1))
            outer.append(jnp.where((place == 0) | (place == WIDTH - 1), v[:, span], moved))
        sides.append(outer)
    for copy in copies[3:]:
        copy.wait()
    for block in range(blocks):
        span = slice(block * LANES, (block + 1) * LANES)
        start = block * ROWS * stride
        rim = jnp.zeros((ROWS, LANES), jnp.float32)
        for level in range(levels):
            low = sides[level][block]
            high = low
            if block > 0:
                low = jnp.where(lane >= LANES - WIDTH, sides[level][block - 1], low)
            else:
                low = jnp.where(lane >= LANES - WIDTH, 0.0, low)
            if block < blocks - 1:
                high = jnp.where(lane < WIDTH, sides[level][block + 1], high)
            else:
                high = jnp.where(lane < WIDTH, 0.0, high)
            for side, picked in enumerate((along_row(low, low_lane), along_row(high, high_lane))):
                rim = jnp.where(row == 2 * level + side, along_lane(picked, x_of), rim)
            sent = (
                velocity[level, :, span],
                base[level, :, span],
                yielded[level, :, span].astype(jnp.float32) * YIELD_WEIGHT,
                FINITE_STEP * (colors[level, :, span] + 1).astype(jnp.float32),
                forcing[level, :, span],
            )
            for field, cells in enumerate(sent):
                lines[pl.ds(start + field * levels + level, ROWS, stride=stride), :] = to_lines(cells, row_of)
        rim = to_lines(rim, row_of)
        lines[pl.ds(start + FIELDS * levels, ROWS, stride=stride), :] = rim


def spread_rows(received, stride, field, levels, store):
    blocks = received.shape[0] // (stride * ROWS)
    for level in range(levels):
        for block in range(blocks):
            rows = received[pl.ds(block * ROWS * stride + field * levels + level, ROWS, stride=stride), :]
            store(block * ROWS * levels + level, rows)


def edge_kernel(levels, received, velocity, viscosity, base, coef, low_edge, high_edge):
    radial = base.shape[0]
    stride = received.shape[0] * levels // radial
    nothing = jnp.zeros((ROWS, LANES), jnp.float32)
    for padded in (velocity, viscosity):
        padded[pl.ds(0, ROWS), :] = nothing
        padded[pl.ds(radial + ROWS, ROWS), :] = nothing

    def store_velocity(first, rows):
        velocity[pl.ds(ROWS + first, ROWS, stride=levels), :] = rows

    def store_base(first, rows):
        base[pl.ds(first, ROWS, stride=levels), :] = rows

    def store_coef(first, rows):
        coef[pl.ds(first, ROWS, stride=levels), :] = rows

    for field, store in enumerate((store_velocity, store_base, store_coef)):
        spread_rows(received, stride, field, levels, store)
    _, group, place = places()
    shift = lax.axis_index("lat") & (ROWS - 1)
    first_lane = shift * WIDTH + place
    last_lane = ((shift + ROWS - 1) & (ROWS - 1)) * WIDTH + place
    for start in range(0, radial, ROWS):
        v = velocity[pl.ds(ROWS + start, ROWS), :]
        eta = base[pl.ds(start, ROWS), :] / (1.0 + coef[pl.ds(start, ROWS), :] * v * v)
        viscosity[pl.ds(ROWS + start, ROWS), :] = eta
        for kind, cells in enumerate((v, eta)):
            for edge, lane_of in ((low_edge, first_lane), (high_edge, last_lane)):
                edge[kind, pl.ds(start // ROWS, 1), :] = along_lane(along_row(cells, lane_of), group)[:1]


def middle_kernel(levels, received, velocity, viscosity, base, coef, out, step, forcing):
    radial = base.shape[0]
    stride = received.shape[0] * levels // radial

    def store_step(first, rows):
        step[pl.ds(first, ROWS, stride=levels), :] = rows

    def store_forcing(first, rows):
        forcing[pl.ds(first, ROWS, stride=levels), :] = rows

    spread_rows(received, stride, 3, levels, store_step)
    spread_rows(received, stride, 4, levels, store_forcing)
    row, group, place = places()
    shift = lax.axis_index("lat") & (ROWS - 1)
    x = (group - shift) & (ROWS - 1)
    first_x, last_x = x == 0, x == ROWS - 1
    first_y, last_y = place == 0, place == WIDTH - 1
    slot = 2 * (row % levels) + jnp.where(first_y, 0, 1)
    v_lane = ((slot + shift) & (ROWS - 1)) * WIDTH + x
    eta_lane = v_lane + ROWS

    def lateral(block, y_rim):
        return (
            jnp.where(first_x, 0.0, pltpu.roll(block, WIDTH, 1)),
            jnp.where(last_x, 0.0, pltpu.roll(block, LANES - WIDTH, 1)),
            jnp.where(first_y, y_rim, pltpu.roll(block, 1, 1)),
            jnp.where(last_y, y_rim, pltpu.roll(block, LANES - 1, 1)),
        )

    for start in range(0, radial, ROWS):
        here = pl.ds(start, ROWS)
        v = velocity[pl.ds(ROWS + start, ROWS), :]
        v_low = velocity[pl.ds(ROWS + start - 1, ROWS), :]
        v_high = velocity[pl.ds(ROWS + start + 1, ROWS), :]
        eta = viscosity[pl.ds(ROWS + start, ROWS), :]
        eta_low = viscosity[pl.ds(ROWS + start - 1, ROWS), :]
        eta_high = viscosity[pl.ds(ROWS + start + 1, ROWS), :]
        b = base[here, :]
        amount = coef[here, :]
        source = start // levels * stride + FIELDS * levels
        rim = received[pl.ds(source, 1), :]
        for later in range(1, ROWS // levels):
            rim = jnp.where(row < later * levels, rim, received[pl.ds(source + later * stride, 1), :])
        near_v = lateral(v, along_row(rim, v_lane)) + (v_low, v_high)
        near_eta = lateral(eta, along_row(rim, eta_lane)) + (eta_low, eta_high)
        value_sum = near_v[0]
        eta_sum = near_eta[0]
        product_sum = near_v[0] * near_eta[0]
        for near_value, near_visc in zip(near_v[1:], near_eta[1:]):
            value_sum = value_sum + near_value
            eta_sum = eta_sum + near_visc
            product_sum = product_sum + near_value * near_visc
        moved = v + step[here, :]
        moved_inverse = 1.0 / (1.0 + amount * moved * moved)
        moved_eta = b * moved_inverse
        slope = -amount * (moved + v) * eta * moved_inverse
        out[0, here, :] = value_sum
        out[1, here, :] = eta_sum
        out[2, here, :] = product_sum
        out[3, here, :] = slope
        out[4, here, :] = b * v - forcing[here, :]
        out[5, here, :] = 3.0 * moved_eta + b
        out[6, here, :] = 0.5 * (slope * (v_low - v) - eta_low - moved_eta)
        out[7, here, :] = 0.5 * (slope * (v_high - v) - eta_high - moved_eta)


def lines_kernel(line_ids, owner_ids, lines_of):
    entries = line_ids.shape[1]
    owner_count, line_count = lines_of.shape
    group = (line_ids[...] // WIDTH + lax.axis_index("lat")) & (ROWS - 1)
    lane_of = group * WIDTH + line_ids[...] % WIDTH
    picks = (lax.broadcasted_iota(jnp.int32, (line_count, entries), 0) == lane_of).astype(jnp.float32)
    owners = (lax.broadcasted_iota(jnp.int32, (owner_count, entries), 0) == owner_ids[...]).astype(jnp.float32)
    lines_of[...] = lax.dot_general(
        owners, picks, (((1,), (1,)), ((), ())), preferred_element_type=jnp.float32
    )


def pencil_kernel(
    levels,
    velocity,
    viscosity,
    middle,
    left,
    right,
    block_diag,
    block_below,
    block_above,
    lines_of,
    out,
    work,
):
    radial = work.shape[1]
    devices = radial // levels
    row, group, place = places()
    x = (group - lax.axis_index("lat")) & (ROWS - 1)
    first_x, last_x = x == 0, x == ROWS - 1
    own_lane = row * WIDTH + place

    def side(kind, start):
        low = along_row(jnp.broadcast_to(left[kind, pl.ds(start // ROWS, 1), :], (ROWS, LANES)), own_lane)
        high = along_row(jnp.broadcast_to(right[kind, pl.ds(start // ROWS, 1), :], (ROWS, LANES)), own_lane)
        return jnp.where(first_x, low, jnp.where(last_x, high, 0.0))

    for start in range(0, radial, ROWS):
        here = pl.ds(start, ROWS)
        v = velocity[pl.ds(ROWS + start, ROWS), :]
        eta = viscosity[pl.ds(ROWS + start, ROWS), :]
        v_rim = side(0, start)
        eta_rim = side(1, start)
        value_sum = middle[0, here, :] + v_rim
        eta_sum = middle[1, here, :] + eta_rim
        product_sum = middle[2, here, :] + v_rim * eta_rim
        spread = 6.0 * v - value_sum
        sensitivity = 0.5 * eta * spread
        work[0, here, :] = sensitivity + 0.5 * (v * eta_sum - product_sum) + middle[4, here, :]
        work[1, here, :] = 0.5 * eta_sum + 0.5 * middle[3, here, :] * spread + middle[5, here, :]
        work[2, here, :] = sensitivity

    residual = work[0]
    half = radial // 2

    def apply_blocks(field):
        head, tail = field[:half], field[half:]
        first = jnp.dot(block_diag[0], head, precision=HIGHEST, preferred_element_type=jnp.float32)
        first = first + jnp.dot(block_above[0], tail, precision=HIGHEST, preferred_element_type=jnp.float32)
        second = jnp.dot(block_diag[1], tail, precision=HIGHEST, preferred_element_type=jnp.float32)
        second = second + jnp.dot(block_below[1], head, precision=HIGHEST, preferred_element_type=jnp.float32)
        return jnp.concatenate([first, second], axis=0)

    initial = apply_blocks(residual)
    level_index = lax.broadcasted_iota(jnp.int32, (radial, LANES), 0)
    from_above = jnp.where(level_index == radial - 1, 0.0, pltpu.roll(middle[6] * initial, radial - 1, 0))
    from_below = jnp.where(level_index == 0, 0.0, pltpu.roll(middle[7] * initial, 1, 0))
    remainder = residual - (work[1] * initial + from_above + from_below)
    correction = initial + apply_blocks(remainder)
    gradient = correction * work[2]
    owned = lax.dot_general(
        lines_of[...],
        gradient,
        (((1,), (1,)), ((), ())),
        precision=HIGHEST,
        preferred_element_type=jnp.float32,
    )
    work[0] = correction
    parts = radial // LANES
    back = levels + parts
    for block in range(devices // ROWS):
        for level in range(levels):
            out[pl.ds(block * ROWS * back + level, ROWS, stride=back), :] = work[
                0, pl.ds(block * ROWS * levels + level, ROWS, stride=levels), :
            ]
        for part in range(parts):
            out[pl.ds(block * ROWS * back + levels + part, ROWS, stride=back), :] = owned[
                block * ROWS : (block + 1) * ROWS, part * LANES : (part + 1) * LANES
            ]


def owned_kernel(levels, received, owned):
    sectors, _, radial = owned.shape
    parts = radial // LANES
    back = levels + parts
    blocks = received.shape[0] // (back * ROWS)
    for part in range(parts):
        total = received[pl.ds(levels + part, ROWS, stride=back), :]
        for block in range(1, blocks):
            total = total + received[pl.ds(block * ROWS * back + levels + part, ROWS, stride=back), :]
        total = jnp.sum(total, axis=0, keepdims=True)
        for sector in range(sectors):
            owned[sector, :, part * LANES : (part + 1) * LANES] = total


def finish_kernel(received, correction):
    levels, rows, width = correction.shape
    blocks = width // LANES
    back = received.shape[0] // (blocks * ROWS)
    row, group, place = places()
    row_of = (group - row) & (ROWS - 1)
    lane_of = ((group + row) & (ROWS - 1)) * WIDTH + place
    for level in range(levels):
        for block in range(blocks):
            lines = received[pl.ds(block * ROWS * back + level, ROWS, stride=back), :]
            correction[level, :, block * LANES : (block + 1) * LANES] = along_row(
                along_lane(lines, row_of), lane_of
            )


def shifted(cells, axis, step):
    count = lax.axis_size(axis)
    return lax.ppermute(cells, axis, [(i, i + step) for i in range(count) if 0 <= i + step < count])


def swapped(rows, parts):
    devices = lax.axis_size("lat")
    sent = rows.reshape(devices, -1, parts, LANES)
    taken = lax.all_to_all(sent, "lat", split_axis=0, concat_axis=0, tiled=True)
    return taken.reshape(rows.shape)


def kernel_call(body, shapes, specs, work, name, scratch=()):
    return pl.pallas_call(
        body,
        out_shape=shapes,
        in_specs=specs,
        out_specs=[VMEM] * len(shapes),
        scratch_shapes=scratch,
        compiler_params=pltpu.CompilerParams(vmem_limit_bytes=32 * MIB),
        cost_estimate=pl.CostEstimate(flops=work[0], bytes_accessed=4 * work[1], transcendentals=0),
        name=name,
    )


def f32(*shape):
    return jax.ShapeDtypeStruct(shape, jnp.float32)


def local(
    velocity,
    base_visc,
    yielded,
    colors,
    forcing,
    block_diag,
    block_below,
    block_above,
    weak_lines,
    weak_owner,
):
    levels, rows, width = velocity.shape
    devices = lax.axis_size("lat")
    sectors = lax.axis_size("sec")
    radial = levels * devices
    cell_count = levels * rows * width
    tile = (levels, rows, width)
    sent_rows = FIELDS * levels + 1
    far = [
        pltpu.with_memory_space_constraint(array, pltpu.HBM)
        for array in (velocity, base_visc, yielded, colors, forcing)
    ]
    (lines,) = kernel_call(
        tile_kernel,
        [f32(devices * sent_rows, LANES)],
        [HBM] * FIELDS,
        (40 * cell_count, 12 * cell_count),
        "tile",
        [pltpu.VMEM(tile, array.dtype) for array in far] + [pltpu.SemaphoreType.DMA((FIELDS,))],
    )(*far)
    lines = swapped(lines, 1)

    (lines_of,) = kernel_call(
        lines_kernel,
        [f32(devices, LANES)],
        [VMEM] * 2,
        (2 * devices * LANES * 64, devices * LANES),
        "lines",
    )(weak_lines.reshape(1, -1), weak_owner.reshape(1, -1))
    back = levels + radial // LANES
    padded = f32(radial + 2 * ROWS, LANES)
    whole = f32(radial, LANES)
    edge = f32(2, radial // ROWS, LANES)

    def edge_body(*refs):
        edge_kernel(levels, *refs)

    def middle_body(*refs):
        middle_kernel(levels, *refs)

    def pencil_body(*refs):
        pencil_kernel(levels, *refs)

    v, eta, base, coef, low_edge, high_edge = kernel_call(
        edge_body,
        [padded, padded, whole, whole, edge, edge],
        [VMEM],
        (10 * cell_count, 7 * cell_count),
        "edges",
    )(lines)
    left = shifted(high_edge, "sec", 1)
    right = shifted(low_edge, "sec", -1)
    (middle,) = kernel_call(
        middle_body,
        [f32(8, radial, LANES)],
        [VMEM] * 5,
        (60 * cell_count, 14 * cell_count),
        "middle",
        [pltpu.VMEM((radial, LANES), jnp.float32), pltpu.VMEM((radial, LANES), jnp.float32)],
    )(lines, v, eta, base, coef)
    (improved,) = kernel_call(
        pencil_body,
        [f32(devices * back, LANES)],
        [VMEM] * 9,
        (24 * radial * radial * LANES, 12 * radial * LANES),
        "pencil",
        [pltpu.VMEM((3, radial, LANES), jnp.float32)],
    )(v, eta, middle, left, right, block_diag, block_below, block_above, lines_of)
    improved = swapped(improved, 2)

    def owned_body(*refs):
        owned_kernel(levels, *refs)

    (owned,) = kernel_call(
        owned_body, [f32(sectors, 1, radial)], [VMEM], (devices * radial, devices * radial), "owned"
    )(improved)
    sums = lax.all_to_all(owned, "sec", split_axis=0, concat_axis=0, tiled=True)
    (correction,) = kernel_call(
        finish_kernel, [f32(*tile)], [VMEM], (4 * cell_count, 3 * cell_count), "finish"
    )(improved)
    weak_grad = jnp.sum(sums, axis=0)
    return (correction, weak_grad)


def solution(mesh):
    return jax.shard_map(
        local,
        mesh=mesh,
        in_specs=(
            P("lat", "sec", None),
            P("lat", "sec", None),
            P("lat", "sec", None),
            P("lat", "sec", None),
            P("lat", "sec", None),
            P(),
            P(),
            P(),
            P("sec", "lat", None),
            P("sec", "lat", None, None),
        ),
        out_specs=(P("lat", "sec", None), P("lat", None)),
        check_vma=False,
    )
```

```python
import jax
import jax.numpy as jnp
from jax import lax
from jax.experimental import pallas as pl
from jax.experimental.pallas import tpu as pltpu
from jax.sharding import PartitionSpec as P

LANES = 128
ROWS = 8
WIDTH = LANES // ROWS
FIELDS = 5
FINITE_STEP = 0.03125
YIELD_WEIGHT = 0.25
VMEM = pl.BlockSpec(memory_space=pltpu.VMEM)
HBM = pl.BlockSpec(memory_space=pltpu.HBM)
MIB = 1024 * 1024


def places():
    row = lax.broadcasted_iota(jnp.int32, (ROWS, LANES), 0)
    lane = lax.broadcasted_iota(jnp.int32, (ROWS, LANES), 1)
    return row, lane // WIDTH, lane % WIDTH


def along_lane(block, row_of):
    return jnp.take_along_axis(block, row_of, axis=0, mode="promise_in_bounds")


def along_row(block, lane_of):
    return jnp.take_along_axis(block, lane_of, axis=1, mode="promise_in_bounds")


def to_lines(block, row_of):
    return along_lane(pltpu.roll(block, 0, 1, stride=WIDTH, stride_axis=0), row_of)


def tile_kernel(
    velocity_far,
    base_far,
    yielded_far,
    colors_far,
    forcing_far,
    lines,
    velocity,
    base,
    yielded,
    colors,
    forcing,
    landed,
):
    arrays = (
        (velocity_far, velocity),
        (base_far, base),
        (yielded_far, yielded),
        (colors_far, colors),
        (forcing_far, forcing),
    )
    copies = [pltpu.make_async_copy(far, near, landed.at[place]) for place, (far, near) in enumerate(arrays)]
    for copy in copies:
        copy.start()
    levels, _, width = velocity.shape
    blocks = width // LANES
    stride = lines.shape[0] // (blocks * ROWS)
    row, group, place = places()
    row_of = (group - row) & (ROWS - 1)
    lane = group * WIDTH + place
    kind = place // ROWS
    low_lane = (group * WIDTH - 1 - kind) & (LANES - 1)
    high_lane = (group * WIDTH + WIDTH + kind) & (LANES - 1)
    x_of = place & (ROWS - 1)
    sides = []
    for copy in copies[:3]:
        copy.wait()
    for level in range(levels):
        v = velocity[level]
        coef = yielded[level].astype(jnp.float32) * YIELD_WEIGHT
        eta = base[level] / (1.0 + coef * v * v)
        outer = []
        for block in range(blocks):
            span = slice(block * LANES, (block + 1) * LANES)
            here = eta[:, span]
            moved = jnp.where(place < ROWS, pltpu.roll(here, 1, 1), pltpu.roll(here, LANES - 1, 1))
            outer.append(jnp.where((place == 0) | (place == WIDTH - 1), v[:, span], moved))
        sides.append(outer)
    for copy in copies[3:]:
        copy.wait()
    for block in range(blocks):
        span = slice(block * LANES, (block + 1) * LANES)
        start = block * ROWS * stride
        rim = jnp.zeros((ROWS, LANES), jnp.float32)
        for level in range(levels):
            low = sides[level][block]
            high = low
            if block > 0:
                low = jnp.where(lane >= LANES - WIDTH, sides[level][block - 1], low)
            else:
                low = jnp.where(lane >= LANES - WIDTH, 0.0, low)
            if block < blocks - 1:
                high = jnp.where(lane < WIDTH, sides[level][block + 1], high)
            else:
                high = jnp.where(lane < WIDTH, 0.0, high)
            for side, picked in enumerate((along_row(low, low_lane), along_row(high, high_lane))):
                rim = jnp.where(row == 2 * level + side, along_lane(picked, x_of), rim)
            sent = (
                velocity[level, :, span],
                base[level, :, span],
                yielded[level, :, span].astype(jnp.float32) * YIELD_WEIGHT,
                FINITE_STEP * (colors[level, :, span] + 1).astype(jnp.float32),
                forcing[level, :, span],
            )
            for field, cells in enumerate(sent):
                lines[pl.ds(start + field * levels + level, ROWS, stride=stride), :] = to_lines(cells, row_of)
        rim = to_lines(rim, row_of)
        lines[pl.ds(start + FIELDS * levels, ROWS, stride=stride), :] = rim


def spread_rows(received, stride, field, levels, store):
    blocks = received.shape[0] // (stride * ROWS)
    for level in range(levels):
        for block in range(blocks):
            rows = received[pl.ds(block * ROWS * stride + field * levels + level, ROWS, stride=stride), :]
            store(block * ROWS * levels + level, rows)


def edge_kernel(levels, received, velocity, viscosity, base, coef, low_edge, high_edge):
    radial = base.shape[0]
    stride = received.shape[0] * levels // radial
    nothing = jnp.zeros((ROWS, LANES), jnp.float32)
    for padded in (velocity, viscosity):
        padded[pl.ds(0, ROWS), :] = nothing
        padded[pl.ds(radial + ROWS, ROWS), :] = nothing

    def store_velocity(first, rows):
        velocity[pl.ds(ROWS + first, ROWS, stride=levels), :] = rows

    def store_base(first, rows):
        base[pl.ds(first, ROWS, stride=levels), :] = rows

    def store_coef(first, rows):
        coef[pl.ds(first, ROWS, stride=levels), :] = rows

    for field, store in enumerate((store_velocity, store_base, store_coef)):
        spread_rows(received, stride, field, levels, store)
    _, group, place = places()
    shift = lax.axis_index("lat") & (ROWS - 1)
    first_lane = shift * WIDTH + place
    last_lane = ((shift + ROWS - 1) & (ROWS - 1)) * WIDTH + place
    for start in range(0, radial, ROWS):
        v = velocity[pl.ds(ROWS + start, ROWS), :]
        eta = base[pl.ds(start, ROWS), :] / (1.0 + coef[pl.ds(start, ROWS), :] * v * v)
        viscosity[pl.ds(ROWS + start, ROWS), :] = eta
        for kind, cells in enumerate((v, eta)):
            for edge, lane_of in ((low_edge, first_lane), (high_edge, last_lane)):
                edge[kind, pl.ds(start // ROWS, 1), :] = along_lane(along_row(cells, lane_of), group)[:1]


def middle_kernel(levels, received, velocity, viscosity, base, coef, out, step, forcing):
    radial = base.shape[0]
    stride = received.shape[0] * levels // radial

    def store_step(first, rows):
        step[pl.ds(first, ROWS, stride=levels), :] = rows

    def store_forcing(first, rows):
        forcing[pl.ds(first, ROWS, stride=levels), :] = rows

    spread_rows(received, stride, 3, levels, store_step)
    spread_rows(received, stride, 4, levels, store_forcing)
    row, group, place = places()
    shift = lax.axis_index("lat") & (ROWS - 1)
    x = (group - shift) & (ROWS - 1)
    first_x, last_x = x == 0, x == ROWS - 1
    first_y, last_y = place == 0, place == WIDTH - 1
    slot = 2 * (row % levels) + jnp.where(first_y, 0, 1)
    v_lane = ((slot + shift) & (ROWS - 1)) * WIDTH + x
    eta_lane = v_lane + ROWS

    def lateral(block, y_rim):
        return (
            jnp.where(first_x, 0.0, pltpu.roll(block, WIDTH, 1)),
            jnp.where(last_x, 0.0, pltpu.roll(block, LANES - WIDTH, 1)),
            jnp.where(first_y, y_rim, pltpu.roll(block, 1, 1)),
            jnp.where(last_y, y_rim, pltpu.roll(block, LANES - 1, 1)),
        )

    for start in range(0, radial, ROWS):
        here = pl.ds(start, ROWS)
        v = velocity[pl.ds(ROWS + start, ROWS), :]
        v_low = velocity[pl.ds(ROWS + start - 1, ROWS), :]
        v_high = velocity[pl.ds(ROWS + start + 1, ROWS), :]
        eta = viscosity[pl.ds(ROWS + start, ROWS), :]
        eta_low = viscosity[pl.ds(ROWS + start - 1, ROWS), :]
        eta_high = viscosity[pl.ds(ROWS + start + 1, ROWS), :]
        b = base[here, :]
        amount = coef[here, :]
        source = start // levels * stride + FIELDS * levels
        rim = received[pl.ds(source, 1), :]
        for later in range(1, ROWS // levels):
            rim = jnp.where(row < later * levels, rim, received[pl.ds(source + later * stride, 1), :])
        near_v = lateral(v, along_row(rim, v_lane)) + (v_low, v_high)
        near_eta = lateral(eta, along_row(rim, eta_lane)) + (eta_low, eta_high)
        value_sum = near_v[0]
        eta_sum = near_eta[0]
        product_sum = near_v[0] * near_eta[0]
        for near_value, near_visc in zip(near_v[1:], near_eta[1:]):
            value_sum = value_sum + near_value
            eta_sum = eta_sum + near_visc
            product_sum = product_sum + near_value * near_visc
        moved = v + step[here, :]
        moved_inverse = 1.0 / (1.0 + amount * moved * moved)
        moved_eta = b * moved_inverse
        slope = -amount * (moved + v) * eta * moved_inverse
        out[0, here, :] = value_sum
        out[1, here, :] = eta_sum
        out[2, here, :] = product_sum
        out[3, here, :] = slope
        out[4, here, :] = b * v - forcing[here, :]
        out[5, here, :] = 3.0 * moved_eta + b
        out[6, here, :] = 0.5 * (slope * (v_low - v) - eta_low - moved_eta)
        out[7, here, :] = 0.5 * (slope * (v_high - v) - eta_high - moved_eta)


def halves(wide):
    high = wide.astype(jnp.bfloat16)
    return high, (wide - high.astype(jnp.float32)).astype(jnp.bfloat16)


def product(left, right, dims):
    return lax.dot_general(left, right, (dims, ((), ())), preferred_element_type=jnp.float32)


def lines_kernel(line_ids, owner_ids, block_diag, block_below, block_above, lines_of, high, low):
    entries = line_ids.shape[1]
    owner_count, line_count = lines_of.shape
    group = (line_ids[...] // WIDTH + lax.axis_index("lat")) & (ROWS - 1)
    lane_of = group * WIDTH + line_ids[...] % WIDTH
    picks = (lax.broadcasted_iota(jnp.int32, (line_count, entries), 0) == lane_of).astype(jnp.bfloat16)
    owners = (lax.broadcasted_iota(jnp.int32, (owner_count, entries), 0) == owner_ids[...]).astype(jnp.bfloat16)
    lines_of[...] = product(owners, picks, ((1,), (1,))).astype(jnp.bfloat16)
    half = block_diag.shape[1]
    quarters = (
        (0, 0, block_diag[0]),
        (0, half, block_above[0]),
        (half, 0, block_below[1]),
        (half, half, block_diag[1]),
    )
    for first_row, first_column, block in quarters:
        place = (pl.ds(first_row, half), pl.ds(first_column, half))
        high[place], low[place] = halves(block)


def pencil_kernel(
    levels,
    velocity,
    viscosity,
    middle,
    left,
    right,
    blocks_high,
    blocks_low,
    lines_of,
    out,
    work,
):
    radial = work.shape[1]
    devices = radial // levels
    row, group, place = places()
    x = (group - lax.axis_index("lat")) & (ROWS - 1)
    first_x, last_x = x == 0, x == ROWS - 1
    own_lane = row * WIDTH + place

    def side(kind, start):
        low = along_row(jnp.broadcast_to(left[kind, pl.ds(start // ROWS, 1), :], (ROWS, LANES)), own_lane)
        high = along_row(jnp.broadcast_to(right[kind, pl.ds(start // ROWS, 1), :], (ROWS, LANES)), own_lane)
        return jnp.where(first_x, low, jnp.where(last_x, high, 0.0))

    for start in range(0, radial, ROWS):
        here = pl.ds(start, ROWS)
        v = velocity[pl.ds(ROWS + start, ROWS), :]
        eta = viscosity[pl.ds(ROWS + start, ROWS), :]
        v_rim = side(0, start)
        eta_rim = side(1, start)
        value_sum = middle[0, here, :] + v_rim
        eta_sum = middle[1, here, :] + eta_rim
        product_sum = middle[2, here, :] + v_rim * eta_rim
        spread = 6.0 * v - value_sum
        sensitivity = 0.5 * eta * spread
        work[0, here, :] = sensitivity + 0.5 * (v * eta_sum - product_sum) + middle[4, here, :]
        work[1, here, :] = 0.5 * eta_sum + 0.5 * middle[3, here, :] * spread + middle[5, here, :]
        work[2, here, :] = sensitivity

    residual = work[0]
    whole = ((1,), (0,))

    def apply_blocks(field):
        high, low = halves(field)
        small = product(blocks_high[...], low, whole) + product(blocks_low[...], high, whole)
        return small + product(blocks_high[...], high, whole)

    initial = apply_blocks(residual)
    level_index = lax.broadcasted_iota(jnp.int32, (radial, LANES), 0)
    from_above = jnp.where(level_index == radial - 1, 0.0, pltpu.roll(middle[6] * initial, radial - 1, 0))
    from_below = jnp.where(level_index == 0, 0.0, pltpu.roll(middle[7] * initial, 1, 0))
    remainder = residual - (work[1] * initial + from_above + from_below)
    correction = initial + apply_blocks(remainder)
    gradient = correction * work[2]
    high, low = halves(gradient)
    over_lines = ((1,), (1,))
    owned = product(lines_of[...], low, over_lines) + product(lines_of[...], high, over_lines)
    work[0] = correction
    parts = radial // LANES
    back = levels + parts
    for block in range(devices // ROWS):
        for level in range(levels):
            out[pl.ds(block * ROWS * back + level, ROWS, stride=back), :] = work[
                0, pl.ds(block * ROWS * levels + level, ROWS, stride=levels), :
            ]
        for part in range(parts):
            out[pl.ds(block * ROWS * back + levels + part, ROWS, stride=back), :] = owned[
                block * ROWS : (block + 1) * ROWS, part * LANES : (part + 1) * LANES
            ]


def owned_kernel(levels, received, owned):
    sectors, _, radial = owned.shape
    parts = radial // LANES
    back = levels + parts
    blocks = received.shape[0] // (back * ROWS)
    for part in range(parts):
        total = received[pl.ds(levels + part, ROWS, stride=back), :]
        for block in range(1, blocks):
            total = total + received[pl.ds(block * ROWS * back + levels + part, ROWS, stride=back), :]
        total = jnp.sum(total, axis=0, keepdims=True)
        for sector in range(sectors):
            owned[sector, :, part * LANES : (part + 1) * LANES] = total


def finish_kernel(received, correction):
    levels, rows, width = correction.shape
    blocks = width // LANES
    back = received.shape[0] // (blocks * ROWS)
    row, group, place = places()
    row_of = (group - row) & (ROWS - 1)
    lane_of = ((group + row) & (ROWS - 1)) * WIDTH + place
    for level in range(levels):
        for block in range(blocks):
            lines = received[pl.ds(block * ROWS * back + level, ROWS, stride=back), :]
            correction[level, :, block * LANES : (block + 1) * LANES] = along_row(
                along_lane(lines, row_of), lane_of
            )


def shifted(cells, axis, step):
    count = lax.axis_size(axis)
    return lax.ppermute(cells, axis, [(i, i + step) for i in range(count) if 0 <= i + step < count])


def swapped(rows, parts):
    devices = lax.axis_size("lat")
    sent = rows.reshape(devices, -1, parts, LANES)
    taken = lax.all_to_all(sent, "lat", split_axis=0, concat_axis=0, tiled=True)
    return taken.reshape(rows.shape)


def kernel_call(body, shapes, specs, work, name, scratch=()):
    return pl.pallas_call(
        body,
        out_shape=shapes,
        in_specs=specs,
        out_specs=[VMEM] * len(shapes),
        scratch_shapes=scratch,
        compiler_params=pltpu.CompilerParams(vmem_limit_bytes=32 * MIB),
        cost_estimate=pl.CostEstimate(flops=work[0], bytes_accessed=4 * work[1], transcendentals=0),
        name=name,
    )


def f32(*shape):
    return jax.ShapeDtypeStruct(shape, jnp.float32)


def local(
    velocity,
    base_visc,
    yielded,
    colors,
    forcing,
    block_diag,
    block_below,
    block_above,
    weak_lines,
    weak_owner,
):
    levels, rows, width = velocity.shape
    devices = lax.axis_size("lat")
    sectors = lax.axis_size("sec")
    radial = levels * devices
    cell_count = levels * rows * width
    tile = (levels, rows, width)
    sent_rows = FIELDS * levels + 1
    far = [
        pltpu.with_memory_space_constraint(array, pltpu.HBM)
        for array in (velocity, base_visc, yielded, colors, forcing)
    ]
    (lines,) = kernel_call(
        tile_kernel,
        [f32(devices * sent_rows, LANES)],
        [HBM] * FIELDS,
        (40 * cell_count, 12 * cell_count),
        "tile",
        [pltpu.VMEM(tile, array.dtype) for array in far] + [pltpu.SemaphoreType.DMA((FIELDS,))],
    )(*far)
    lines = swapped(lines, 1)

    def b16(*shape):
        return jax.ShapeDtypeStruct(shape, jnp.bfloat16)

    lines_of, blocks_high, blocks_low = kernel_call(
        lines_kernel,
        [b16(devices, LANES), b16(radial, radial), b16(radial, radial)],
        [VMEM] * 5,
        (2 * devices * LANES * 64, 3 * radial * radial),
        "lines",
    )(weak_lines.reshape(1, -1), weak_owner.reshape(1, -1), block_diag, block_below, block_above)
    back = levels + radial // LANES
    padded = f32(radial + 2 * ROWS, LANES)
    whole = f32(radial, LANES)
    edge = f32(2, radial // ROWS, LANES)

    def edge_body(*refs):
        edge_kernel(levels, *refs)

    def middle_body(*refs):
        middle_kernel(levels, *refs)

    def pencil_body(*refs):
        pencil_kernel(levels, *refs)

    v, eta, base, coef, low_edge, high_edge = kernel_call(
        edge_body,
        [padded, padded, whole, whole, edge, edge],
        [VMEM],
        (10 * cell_count, 7 * cell_count),
        "edges",
    )(lines)
    left = shifted(high_edge, "sec", 1)
    right = shifted(low_edge, "sec", -1)
    (middle,) = kernel_call(
        middle_body,
        [f32(8, radial, LANES)],
        [VMEM] * 5,
        (60 * cell_count, 14 * cell_count),
        "middle",
        [pltpu.VMEM((radial, LANES), jnp.float32), pltpu.VMEM((radial, LANES), jnp.float32)],
    )(lines, v, eta, base, coef)
    (improved,) = kernel_call(
        pencil_body,
        [f32(devices * back, LANES)],
        [VMEM] * 8,
        (24 * radial * radial * LANES, 12 * radial * LANES),
        "pencil",
        [pltpu.VMEM((3, radial, LANES), jnp.float32)],
    )(v, eta, middle, left, right, blocks_high, blocks_low, lines_of)
    improved = swapped(improved, 2)

    def owned_body(*refs):
        owned_kernel(levels, *refs)

    (owned,) = kernel_call(
        owned_body, [f32(sectors, 1, radial)], [VMEM], (devices * radial, devices * radial), "owned"
    )(improved)
    sums = lax.all_to_all(owned, "sec", split_axis=0, concat_axis=0, tiled=True)
    (correction,) = kernel_call(
        finish_kernel, [f32(*tile)], [VMEM], (4 * cell_count, 3 * cell_count), "finish"
    )(improved)
    weak_grad = jnp.sum(sums, axis=0)
    return (correction, weak_grad)


def solution(mesh):
    return jax.shard_map(
        local,
        mesh=mesh,
        in_specs=(
            P("lat", "sec", None),
            P("lat", "sec", None),
            P("lat", "sec", None),
            P("lat", "sec", None),
            P("lat", "sec", None),
            P(),
            P(),
            P(),
            P("sec", "lat", None),
            P("sec", "lat", None, None),
        ),
        out_specs=(P("lat", "sec", None), P("lat", None)),
        check_vma=False,
    )
```

```python
import jax
import jax.numpy as jnp
from jax import lax
from jax.experimental import pallas as pl
from jax.experimental.pallas import tpu as pltpu
from jax.sharding import PartitionSpec as P

LANES = 128
ROWS = 8
WIDTH = LANES // ROWS
FIELDS = 5
FINITE_STEP = 0.03125
YIELD_WEIGHT = 0.25
VMEM = pl.BlockSpec(memory_space=pltpu.VMEM)
HBM = pl.BlockSpec(memory_space=pltpu.HBM)
MIB = 1024 * 1024


def places():
    row = lax.broadcasted_iota(jnp.int32, (ROWS, LANES), 0)
    lane = lax.broadcasted_iota(jnp.int32, (ROWS, LANES), 1)
    return row, lane // WIDTH, lane % WIDTH


def along_lane(block, row_of):
    return jnp.take_along_axis(block, row_of, axis=0, mode="promise_in_bounds")


def along_row(block, lane_of):
    return jnp.take_along_axis(block, lane_of, axis=1, mode="promise_in_bounds")


def to_lines(block, row_of):
    return along_lane(pltpu.roll(block, 0, 1, stride=WIDTH, stride_axis=0), row_of)


def tile_kernel(
    velocity_far,
    base_far,
    yielded_far,
    colors_far,
    forcing_far,
    lines,
    velocity,
    base,
    yielded,
    colors,
    forcing,
    landed,
):
    arrays = (
        (velocity_far, velocity),
        (base_far, base),
        (yielded_far, yielded),
        (colors_far, colors),
        (forcing_far, forcing),
    )
    copies = [pltpu.make_async_copy(far, near, landed.at[place]) for place, (far, near) in enumerate(arrays)]
    for copy in copies:
        copy.start()
    levels, _, width = velocity.shape
    blocks = width // LANES
    stride = lines.shape[0] // (blocks * ROWS)
    row, group, place = places()
    row_of = (group - row) & (ROWS - 1)
    lane = group * WIDTH + place
    kind = place // ROWS
    low_lane = (group * WIDTH - 1 - kind) & (LANES - 1)
    high_lane = (group * WIDTH + WIDTH + kind) & (LANES - 1)
    x_of = place & (ROWS - 1)
    sides = []
    for copy in copies[:3]:
        copy.wait()
    for level in range(levels):
        v = velocity[level]
        coef = yielded[level].astype(jnp.float32) * YIELD_WEIGHT
        eta = base[level] / (1.0 + coef * v * v)
        outer = []
        for block in range(blocks):
            span = slice(block * LANES, (block + 1) * LANES)
            here = eta[:, span]
            moved = jnp.where(place < ROWS, pltpu.roll(here, 1, 1), pltpu.roll(here, LANES - 1, 1))
            outer.append(jnp.where((place == 0) | (place == WIDTH - 1), v[:, span], moved))
        sides.append(outer)

    def send(field, level, block, cells):
        start = block * ROWS * stride + field * levels + level
        lines[pl.ds(start, ROWS, stride=stride), :] = to_lines(cells, row_of)

    for block in range(blocks):
        span = slice(block * LANES, (block + 1) * LANES)
        rim = jnp.zeros((ROWS, LANES), jnp.float32)
        for level in range(levels):
            low = sides[level][block]
            high = low
            if block > 0:
                low = jnp.where(lane >= LANES - WIDTH, sides[level][block - 1], low)
            else:
                low = jnp.where(lane >= LANES - WIDTH, 0.0, low)
            if block < blocks - 1:
                high = jnp.where(lane < WIDTH, sides[level][block + 1], high)
            else:
                high = jnp.where(lane < WIDTH, 0.0, high)
            for side, picked in enumerate((along_row(low, low_lane), along_row(high, high_lane))):
                rim = jnp.where(row == 2 * level + side, along_lane(picked, x_of), rim)
            send(0, level, block, velocity[level, :, span])
            send(1, level, block, base[level, :, span])
            send(2, level, block, yielded[level, :, span].astype(jnp.float32) * YIELD_WEIGHT)
        send(FIELDS, 0, block, rim)
    for copy in copies[3:]:
        copy.wait()
    for block in range(blocks):
        span = slice(block * LANES, (block + 1) * LANES)
        for level in range(levels):
            send(3, level, block, FINITE_STEP * (colors[level, :, span] + 1).astype(jnp.float32))
            send(4, level, block, forcing[level, :, span])


def spread_rows(received, stride, field, levels, store):
    blocks = received.shape[0] // (stride * ROWS)
    for level in range(levels):
        for block in range(blocks):
            rows = received[pl.ds(block * ROWS * stride + field * levels + level, ROWS, stride=stride), :]
            store(block * ROWS * levels + level, rows)


def edge_kernel(levels, received, velocity, viscosity, base, coef, inner_edge, outer_edge):
    radial = base.shape[0]
    stride = received.shape[0] * levels // radial
    nothing = jnp.zeros((ROWS, LANES), jnp.float32)
    for padded in (velocity, viscosity):
        padded[pl.ds(0, ROWS), :] = nothing
        padded[pl.ds(radial + ROWS, ROWS), :] = nothing

    def store_velocity(first, rows):
        velocity[pl.ds(ROWS + first, ROWS, stride=levels), :] = rows

    def store_base(first, rows):
        base[pl.ds(first, ROWS, stride=levels), :] = rows

    def store_coef(first, rows):
        coef[pl.ds(first, ROWS, stride=levels), :] = rows

    for field, store in enumerate((store_velocity, store_base, store_coef)):
        spread_rows(received, stride, field, levels, store)
    _, group, place = places()
    shift = lax.axis_index("lat") & (ROWS - 1)
    odd = lax.axis_index("sec") & 1
    inner_lane = ((shift + (1 - odd) * (ROWS - 1)) & (ROWS - 1)) * WIDTH + place
    outer_lane = ((shift + odd * (ROWS - 1)) & (ROWS - 1)) * WIDTH + place
    for start in range(0, radial, ROWS):
        v = velocity[pl.ds(ROWS + start, ROWS), :]
        eta = base[pl.ds(start, ROWS), :] / (1.0 + coef[pl.ds(start, ROWS), :] * v * v)
        viscosity[pl.ds(ROWS + start, ROWS), :] = eta
        for kind, cells in enumerate((v, eta)):
            for edge, lane_of in ((inner_edge, inner_lane), (outer_edge, outer_lane)):
                edge[kind, pl.ds(start // ROWS, 1), :] = along_lane(along_row(cells, lane_of), group)[:1]


def middle_kernel(levels, received, velocity, viscosity, base, coef, out, step, forcing):
    radial = base.shape[0]
    stride = received.shape[0] * levels // radial

    def store_step(first, rows):
        step[pl.ds(first, ROWS, stride=levels), :] = rows

    def store_forcing(first, rows):
        forcing[pl.ds(first, ROWS, stride=levels), :] = rows

    spread_rows(received, stride, 3, levels, store_step)
    spread_rows(received, stride, 4, levels, store_forcing)
    row, group, place = places()
    shift = lax.axis_index("lat") & (ROWS - 1)
    x = (group - shift) & (ROWS - 1)
    first_x, last_x = x == 0, x == ROWS - 1
    first_y, last_y = place == 0, place == WIDTH - 1
    slot = 2 * (row % levels) + jnp.where(first_y, 0, 1)
    v_lane = ((slot + shift) & (ROWS - 1)) * WIDTH + x
    eta_lane = v_lane + ROWS

    def lateral(block, y_rim):
        return (
            jnp.where(first_x, 0.0, pltpu.roll(block, WIDTH, 1)),
            jnp.where(last_x, 0.0, pltpu.roll(block, LANES - WIDTH, 1)),
            jnp.where(first_y, y_rim, pltpu.roll(block, 1, 1)),
            jnp.where(last_y, y_rim, pltpu.roll(block, LANES - 1, 1)),
        )

    for start in range(0, radial, ROWS):
        here = pl.ds(start, ROWS)
        v = velocity[pl.ds(ROWS + start, ROWS), :]
        v_low = velocity[pl.ds(ROWS + start - 1, ROWS), :]
        v_high = velocity[pl.ds(ROWS + start + 1, ROWS), :]
        eta = viscosity[pl.ds(ROWS + start, ROWS), :]
        eta_low = viscosity[pl.ds(ROWS + start - 1, ROWS), :]
        eta_high = viscosity[pl.ds(ROWS + start + 1, ROWS), :]
        b = base[here, :]
        amount = coef[here, :]
        source = start // levels * stride + FIELDS * levels
        rim = received[pl.ds(source, 1), :]
        for later in range(1, ROWS // levels):
            rim = jnp.where(row < later * levels, rim, received[pl.ds(source + later * stride, 1), :])
        near_v = lateral(v, along_row(rim, v_lane)) + (v_low, v_high)
        near_eta = lateral(eta, along_row(rim, eta_lane)) + (eta_low, eta_high)
        value_sum = near_v[0]
        eta_sum = near_eta[0]
        product_sum = near_v[0] * near_eta[0]
        for near_value, near_visc in zip(near_v[1:], near_eta[1:]):
            value_sum = value_sum + near_value
            eta_sum = eta_sum + near_visc
            product_sum = product_sum + near_value * near_visc
        moved = v + step[here, :]
        moved_inverse = 1.0 / (1.0 + amount * moved * moved)
        moved_eta = b * moved_inverse
        slope = -amount * (moved + v) * eta * moved_inverse
        out[0, here, :] = value_sum
        out[1, here, :] = eta_sum
        out[2, here, :] = product_sum
        out[3, here, :] = slope
        out[4, here, :] = b * v - forcing[here, :]
        out[5, here, :] = 3.0 * moved_eta + b
        out[6, here, :] = 0.5 * (slope * (v_low - v) - eta_low - moved_eta)
        out[7, here, :] = 0.5 * (slope * (v_high - v) - eta_high - moved_eta)


def halves(wide):
    high = wide.astype(jnp.bfloat16)
    return high, (wide - high.astype(jnp.float32)).astype(jnp.bfloat16)


def product(left, right, dims):
    return lax.dot_general(left, right, (dims, ((), ())), preferred_element_type=jnp.float32)


def lines_kernel(line_ids, owner_ids, block_diag, block_below, block_above, lines_of, high, low):
    entries = line_ids.shape[1]
    owner_count, line_count = lines_of.shape
    group = (line_ids[...] // WIDTH + lax.axis_index("lat")) & (ROWS - 1)
    lane_of = group * WIDTH + line_ids[...] % WIDTH
    picks = (lax.broadcasted_iota(jnp.int32, (line_count, entries), 0) == lane_of).astype(jnp.bfloat16)
    owners = (lax.broadcasted_iota(jnp.int32, (owner_count, entries), 0) == owner_ids[...]).astype(jnp.bfloat16)
    lines_of[...] = product(owners, picks, ((1,), (1,))).astype(jnp.bfloat16)
    half = block_diag.shape[1]
    quarters = (
        (0, 0, block_diag[0]),
        (0, half, block_above[0]),
        (half, 0, block_below[1]),
        (half, half, block_diag[1]),
    )
    for first_row, first_column, block in quarters:
        place = (pl.ds(first_row, half), pl.ds(first_column, half))
        high[place], low[place] = halves(block)


def pencil_kernel(
    levels,
    velocity,
    viscosity,
    middle,
    inner,
    outer,
    blocks_high,
    blocks_low,
    lines_of,
    out,
    work,
):
    radial = work.shape[1]
    devices = radial // levels
    row, group, place = places()
    x = (group - lax.axis_index("lat")) & (ROWS - 1)
    own_lane = row * WIDTH + place

    odd = lax.axis_index("sec") & 1
    inner_x, outer_x = x == (1 - odd) * (ROWS - 1), x == odd * (ROWS - 1)

    def side(kind, start):
        near = along_row(jnp.broadcast_to(inner[kind, pl.ds(start // ROWS, 1), :], (ROWS, LANES)), own_lane)
        far = along_row(jnp.broadcast_to(outer[kind, pl.ds(start // ROWS, 1), :], (ROWS, LANES)), own_lane)
        return jnp.where(inner_x, near, jnp.where(outer_x, far, 0.0))

    for start in range(0, radial, ROWS):
        here = pl.ds(start, ROWS)
        v = velocity[pl.ds(ROWS + start, ROWS), :]
        eta = viscosity[pl.ds(ROWS + start, ROWS), :]
        v_rim = side(0, start)
        eta_rim = side(1, start)
        value_sum = middle[0, here, :] + v_rim
        eta_sum = middle[1, here, :] + eta_rim
        product_sum = middle[2, here, :] + v_rim * eta_rim
        spread = 6.0 * v - value_sum
        sensitivity = 0.5 * eta * spread
        work[0, here, :] = sensitivity + 0.5 * (v * eta_sum - product_sum) + middle[4, here, :]
        work[1, here, :] = 0.5 * eta_sum + 0.5 * middle[3, here, :] * spread + middle[5, here, :]
        work[2, here, :] = sensitivity

    residual = work[0]
    whole = ((1,), (0,))

    def apply_blocks(field):
        high, low = halves(field)
        small = product(blocks_high[...], low, whole) + product(blocks_low[...], high, whole)
        return small + product(blocks_high[...], high, whole)

    initial = apply_blocks(residual)
    level_index = lax.broadcasted_iota(jnp.int32, (radial, LANES), 0)
    from_above = jnp.where(level_index == radial - 1, 0.0, pltpu.roll(middle[6] * initial, radial - 1, 0))
    from_below = jnp.where(level_index == 0, 0.0, pltpu.roll(middle[7] * initial, 1, 0))
    remainder = residual - (work[1] * initial + from_above + from_below)
    correction = initial + apply_blocks(remainder)
    gradient = correction * work[2]
    high, low = halves(gradient)
    over_lines = ((1,), (1,))
    owned = product(lines_of[...], low, over_lines) + product(lines_of[...], high, over_lines)
    work[0] = correction
    parts = radial // LANES
    back = levels + parts
    for block in range(devices // ROWS):
        for level in range(levels):
            out[pl.ds(block * ROWS * back + level, ROWS, stride=back), :] = work[
                0, pl.ds(block * ROWS * levels + level, ROWS, stride=levels), :
            ]
        for part in range(parts):
            out[pl.ds(block * ROWS * back + levels + part, ROWS, stride=back), :] = owned[
                block * ROWS : (block + 1) * ROWS, part * LANES : (part + 1) * LANES
            ]


def owned_kernel(levels, received, owned):
    sectors, _, radial = owned.shape
    parts = radial // LANES
    back = levels + parts
    blocks = received.shape[0] // (back * ROWS)
    for part in range(parts):
        total = received[pl.ds(levels + part, ROWS, stride=back), :]
        for block in range(1, blocks):
            total = total + received[pl.ds(block * ROWS * back + levels + part, ROWS, stride=back), :]
        total = jnp.sum(total, axis=0, keepdims=True)
        for sector in range(sectors):
            owned[sector, :, part * LANES : (part + 1) * LANES] = total


def finish_kernel(received, correction):
    levels, rows, width = correction.shape
    blocks = width // LANES
    back = received.shape[0] // (blocks * ROWS)
    row, group, place = places()
    row_of = (group - row) & (ROWS - 1)
    lane_of = ((group + row) & (ROWS - 1)) * WIDTH + place
    for level in range(levels):
        for block in range(blocks):
            lines = received[pl.ds(block * ROWS * back + level, ROWS, stride=back), :]
            correction[level, :, block * LANES : (block + 1) * LANES] = along_row(
                along_lane(lines, row_of), lane_of
            )


def swapped(rows, parts):
    devices = lax.axis_size("lat")
    sent = rows.reshape(devices, -1, parts, LANES)
    taken = lax.all_to_all(sent, "lat", split_axis=0, concat_axis=0, tiled=True)
    return taken.reshape(rows.shape)


def kernel_call(body, shapes, specs, work, name, scratch=()):
    return pl.pallas_call(
        body,
        out_shape=shapes,
        in_specs=specs,
        out_specs=[VMEM] * len(shapes),
        scratch_shapes=scratch,
        compiler_params=pltpu.CompilerParams(vmem_limit_bytes=32 * MIB),
        cost_estimate=pl.CostEstimate(flops=work[0], bytes_accessed=4 * work[1], transcendentals=0),
        name=name,
    )


def f32(*shape):
    return jax.ShapeDtypeStruct(shape, jnp.float32)


def local(
    velocity,
    base_visc,
    yielded,
    colors,
    forcing,
    block_diag,
    block_below,
    block_above,
    weak_lines,
    weak_owner,
):
    levels, rows, width = velocity.shape
    devices = lax.axis_size("lat")
    sectors = lax.axis_size("sec")
    radial = levels * devices
    cell_count = levels * rows * width
    tile = (levels, rows, width)
    sent_rows = FIELDS * levels + 1
    far = [
        pltpu.with_memory_space_constraint(array, pltpu.HBM)
        for array in (velocity, base_visc, yielded, colors, forcing)
    ]
    (lines,) = kernel_call(
        tile_kernel,
        [f32(devices * sent_rows, LANES)],
        [HBM] * FIELDS,
        (40 * cell_count, 12 * cell_count),
        "tile",
        [pltpu.VMEM(tile, array.dtype) for array in far] + [pltpu.SemaphoreType.DMA((FIELDS,))],
    )(*far)
    lines = swapped(lines, 1)

    def b16(*shape):
        return jax.ShapeDtypeStruct(shape, jnp.bfloat16)

    lines_of, blocks_high, blocks_low = kernel_call(
        lines_kernel,
        [b16(devices, LANES), b16(radial, radial), b16(radial, radial)],
        [VMEM] * 5,
        (2 * devices * LANES * 64, 3 * radial * radial),
        "lines",
    )(weak_lines.reshape(1, -1), weak_owner.reshape(1, -1), block_diag, block_below, block_above)
    back = levels + radial // LANES
    padded = f32(radial + 2 * ROWS, LANES)
    whole = f32(radial, LANES)
    edge = f32(2, radial // ROWS, LANES)

    def edge_body(*refs):
        edge_kernel(levels, *refs)

    def middle_body(*refs):
        middle_kernel(levels, *refs)

    def pencil_body(*refs):
        pencil_kernel(levels, *refs)

    v, eta, base, coef, inner_edge, outer_edge = kernel_call(
        edge_body,
        [padded, padded, whole, whole, edge, edge],
        [VMEM],
        (10 * cell_count, 7 * cell_count),
        "edges",
    )(lines)
    inner = lax.ppermute(inner_edge, "sec", [(i, i ^ 1) for i in range(sectors)])
    outer = lax.ppermute(outer_edge, "sec", [(i, i + 1 if i % 2 else i - 1) for i in range(1, sectors - 1)])
    (middle,) = kernel_call(
        middle_body,
        [f32(8, radial, LANES)],
        [VMEM] * 5,
        (60 * cell_count, 14 * cell_count),
        "middle",
        [pltpu.VMEM((radial, LANES), jnp.float32), pltpu.VMEM((radial, LANES), jnp.float32)],
    )(lines, v, eta, base, coef)
    (improved,) = kernel_call(
        pencil_body,
        [f32(devices * back, LANES)],
        [VMEM] * 8,
        (24 * radial * radial * LANES, 12 * radial * LANES),
        "pencil",
        [pltpu.VMEM((3, radial, LANES), jnp.float32)],
    )(v, eta, middle, inner, outer, blocks_high, blocks_low, lines_of)
    improved = swapped(improved, 2)

    def owned_body(*refs):
        owned_kernel(levels, *refs)

    (owned,) = kernel_call(
        owned_body, [f32(sectors, 1, radial)], [VMEM], (devices * radial, devices * radial), "owned"
    )(improved)
    sums = lax.all_to_all(owned, "sec", split_axis=0, concat_axis=0, tiled=True)
    (correction,) = kernel_call(
        finish_kernel, [f32(*tile)], [VMEM], (4 * cell_count, 3 * cell_count), "finish"
    )(improved)
    weak_grad = jnp.sum(sums, axis=0)
    return (correction, weak_grad)


def solution(mesh):
    return jax.shard_map(
        local,
        mesh=mesh,
        in_specs=(
            P("lat", "sec", None),
            P("lat", "sec", None),
            P("lat", "sec", None),
            P("lat", "sec", None),
            P("lat", "sec", None),
            P(),
            P(),
            P(),
            P("sec", "lat", None),
            P("sec", "lat", None, None),
        ),
        out_specs=(P("lat", "sec", None), P("lat", None)),
        check_vma=False,
    )
```

```python
import jax
import jax.numpy as jnp
from jax import lax
from jax.experimental import pallas as pl
from jax.experimental.pallas import tpu as pltpu
from jax.sharding import PartitionSpec as P

LANES = 128
ROWS = 8
WIDTH = LANES // ROWS
FIELDS = 5
FINITE_STEP = 0.03125
YIELD_WEIGHT = 0.25
VMEM = pl.BlockSpec(memory_space=pltpu.VMEM)
HBM = pl.BlockSpec(memory_space=pltpu.HBM)
MIB = 1024 * 1024


def places():
    row = lax.broadcasted_iota(jnp.int32, (ROWS, LANES), 0)
    lane = lax.broadcasted_iota(jnp.int32, (ROWS, LANES), 1)
    return row, lane // WIDTH, lane % WIDTH


def along_lane(block, row_of):
    return jnp.take_along_axis(block, row_of, axis=0, mode="promise_in_bounds")


def along_row(block, lane_of):
    return jnp.take_along_axis(block, lane_of, axis=1, mode="promise_in_bounds")


def to_lines(block, row_of):
    return along_lane(pltpu.roll(block, 0, 1, stride=WIDTH, stride_axis=0), row_of)


def tile_kernel(
    velocity_far,
    base_far,
    yielded_far,
    colors_far,
    forcing_far,
    lines,
    velocity,
    base,
    yielded,
    colors,
    forcing,
    landed,
):
    arrays = (
        (velocity_far, velocity),
        (base_far, base),
        (yielded_far, yielded),
        (colors_far, colors),
        (forcing_far, forcing),
    )
    copies = [pltpu.make_async_copy(far, near, landed.at[place]) for place, (far, near) in enumerate(arrays)]
    for copy in copies:
        copy.start()
    levels, _, width = velocity.shape
    blocks = width // LANES
    stride = lines.shape[0] // (blocks * ROWS)
    row, group, place = places()
    row_of = (group - row) & (ROWS - 1)
    lane = group * WIDTH + place
    kind = place // ROWS
    low_lane = (group * WIDTH - 1 - kind) & (LANES - 1)
    high_lane = (group * WIDTH + WIDTH + kind) & (LANES - 1)
    x_of = place & (ROWS - 1)
    sides = []
    for copy in copies[:3]:
        copy.wait()
    for level in range(levels):
        v = velocity[level]
        coef = yielded[level].astype(jnp.float32) * YIELD_WEIGHT
        eta = base[level] / (1.0 + coef * v * v)
        outer = []
        for block in range(blocks):
            span = slice(block * LANES, (block + 1) * LANES)
            here = eta[:, span]
            moved = jnp.where(place < ROWS, pltpu.roll(here, 1, 1), pltpu.roll(here, LANES - 1, 1))
            outer.append(jnp.where((place == 0) | (place == WIDTH - 1), v[:, span], moved))
        sides.append(outer)

    def send(field, level, block, cells):
        start = block * ROWS * stride + field * levels + level
        lines[pl.ds(start, ROWS, stride=stride), :] = to_lines(cells, row_of)

    for block in range(blocks):
        span = slice(block * LANES, (block + 1) * LANES)
        rim = jnp.zeros((ROWS, LANES), jnp.float32)
        for level in range(levels):
            low = sides[level][block]
            high = low
            if block > 0:
                low = jnp.where(lane >= LANES - WIDTH, sides[level][block - 1], low)
            else:
                low = jnp.where(lane >= LANES - WIDTH, 0.0, low)
            if block < blocks - 1:
                high = jnp.where(lane < WIDTH, sides[level][block + 1], high)
            else:
                high = jnp.where(lane < WIDTH, 0.0, high)
            for side, picked in enumerate((along_row(low, low_lane), along_row(high, high_lane))):
                rim = jnp.where(row == 2 * level + side, along_lane(picked, x_of), rim)
            send(0, level, block, velocity[level, :, span])
            send(1, level, block, base[level, :, span])
            send(2, level, block, yielded[level, :, span].astype(jnp.float32) * YIELD_WEIGHT)
        send(FIELDS, 0, block, rim)
    for copy in copies[3:]:
        copy.wait()
    for block in range(blocks):
        span = slice(block * LANES, (block + 1) * LANES)
        for level in range(levels):
            send(3, level, block, FINITE_STEP * (colors[level, :, span] + 1).astype(jnp.float32))
            send(4, level, block, forcing[level, :, span])


def spread_rows(received, stride, field, levels, store):
    blocks = received.shape[0] // (stride * ROWS)
    for level in range(levels):
        for block in range(blocks):
            rows = received[pl.ds(block * ROWS * stride + field * levels + level, ROWS, stride=stride), :]
            store(block * ROWS * levels + level, rows)


def edge_kernel(levels, received, velocity, viscosity, base, coef, inner_edge, outer_edge):
    radial = base.shape[0]
    stride = received.shape[0] * levels // radial
    nothing = jnp.zeros((ROWS, LANES), jnp.float32)
    for padded in (velocity, viscosity):
        padded[pl.ds(0, ROWS), :] = nothing
        padded[pl.ds(radial + ROWS, ROWS), :] = nothing

    def store_velocity(first, rows):
        velocity[pl.ds(ROWS + first, ROWS, stride=levels), :] = rows

    def store_base(first, rows):
        base[pl.ds(first, ROWS, stride=levels), :] = rows

    def store_coef(first, rows):
        coef[pl.ds(first, ROWS, stride=levels), :] = rows

    for field, store in enumerate((store_velocity, store_base, store_coef)):
        spread_rows(received, stride, field, levels, store)
    _, group, place = places()
    shift = lax.axis_index("lat") & (ROWS - 1)
    odd = lax.axis_index("sec") & 1
    inner_lane = ((shift + (1 - odd) * (ROWS - 1)) & (ROWS - 1)) * WIDTH + place
    outer_lane = ((shift + odd * (ROWS - 1)) & (ROWS - 1)) * WIDTH + place
    for start in range(0, radial, ROWS):
        v = velocity[pl.ds(ROWS + start, ROWS), :]
        eta = base[pl.ds(start, ROWS), :] / (1.0 + coef[pl.ds(start, ROWS), :] * v * v)
        viscosity[pl.ds(ROWS + start, ROWS), :] = eta
        for kind, cells in enumerate((v, eta)):
            for edge, lane_of in ((inner_edge, inner_lane), (outer_edge, outer_lane)):
                edge[kind, pl.ds(start // ROWS, 1), :] = along_lane(along_row(cells, lane_of), group)[:1]


def middle_kernel(levels, received, velocity, viscosity, base, coef, out, step, forcing):
    radial = base.shape[0]
    stride = received.shape[0] * levels // radial

    def store_step(first, rows):
        step[pl.ds(first, ROWS, stride=levels), :] = rows

    def store_forcing(first, rows):
        forcing[pl.ds(first, ROWS, stride=levels), :] = rows

    spread_rows(received, stride, 3, levels, store_step)
    spread_rows(received, stride, 4, levels, store_forcing)
    row, group, place = places()
    shift = lax.axis_index("lat") & (ROWS - 1)
    x = (group - shift) & (ROWS - 1)
    first_x, last_x = x == 0, x == ROWS - 1
    first_y, last_y = place == 0, place == WIDTH - 1
    slot = 2 * (row % levels) + jnp.where(first_y, 0, 1)
    v_lane = ((slot + shift) & (ROWS - 1)) * WIDTH + x
    eta_lane = v_lane + ROWS

    def lateral(block, y_rim):
        return (
            jnp.where(first_x, 0.0, pltpu.roll(block, WIDTH, 1)),
            jnp.where(last_x, 0.0, pltpu.roll(block, LANES - WIDTH, 1)),
            jnp.where(first_y, y_rim, pltpu.roll(block, 1, 1)),
            jnp.where(last_y, y_rim, pltpu.roll(block, LANES - 1, 1)),
        )

    for start in range(0, radial, ROWS):
        here = pl.ds(start, ROWS)
        v = velocity[pl.ds(ROWS + start, ROWS), :]
        v_low = velocity[pl.ds(ROWS + start - 1, ROWS), :]
        v_high = velocity[pl.ds(ROWS + start + 1, ROWS), :]
        eta = viscosity[pl.ds(ROWS + start, ROWS), :]
        eta_low = viscosity[pl.ds(ROWS + start - 1, ROWS), :]
        eta_high = viscosity[pl.ds(ROWS + start + 1, ROWS), :]
        b = base[here, :]
        amount = coef[here, :]
        source = start // levels * stride + FIELDS * levels
        rim = received[pl.ds(source, 1), :]
        for later in range(1, ROWS // levels):
            rim = jnp.where(row < later * levels, rim, received[pl.ds(source + later * stride, 1), :])
        near_v = lateral(v, along_row(rim, v_lane)) + (v_low, v_high)
        near_eta = lateral(eta, along_row(rim, eta_lane)) + (eta_low, eta_high)
        value_sum = near_v[0]
        eta_sum = near_eta[0]
        product_sum = near_v[0] * near_eta[0]
        for near_value, near_visc in zip(near_v[1:], near_eta[1:]):
            value_sum = value_sum + near_value
            eta_sum = eta_sum + near_visc
            product_sum = product_sum + near_value * near_visc
        moved = v + step[here, :]
        moved_inverse = 1.0 / (1.0 + amount * moved * moved)
        moved_eta = b * moved_inverse
        slope = -amount * (moved + v) * eta * moved_inverse
        out[0, here, :] = value_sum
        out[1, here, :] = eta_sum
        out[2, here, :] = product_sum
        out[3, here, :] = slope
        out[4, here, :] = b * v - forcing[here, :]
        out[5, here, :] = 3.0 * moved_eta + b
        out[6, here, :] = 0.5 * (slope * (v_low - v) - eta_low - moved_eta)
        out[7, here, :] = 0.5 * (slope * (v_high - v) - eta_high - moved_eta)


def halves(wide):
    high = wide.astype(jnp.bfloat16)
    return high, (wide - high.astype(jnp.float32)).astype(jnp.bfloat16)


def product(left, right, dims):
    return lax.dot_general(left, right, (dims, ((), ())), preferred_element_type=jnp.float32)


def lines_kernel(line_ids, owner_ids, block_diag, block_below, block_above, lines_of, high, low):
    entries = line_ids.shape[1]
    owner_count, line_count = lines_of.shape
    group = (line_ids[...] // WIDTH + lax.axis_index("lat")) & (ROWS - 1)
    lane_of = group * WIDTH + line_ids[...] % WIDTH
    picks = (lax.broadcasted_iota(jnp.int32, (line_count, entries), 0) == lane_of).astype(jnp.bfloat16)
    owners = (lax.broadcasted_iota(jnp.int32, (owner_count, entries), 0) == owner_ids[...]).astype(jnp.bfloat16)
    lines_of[...] = product(owners, picks, ((1,), (1,))).astype(jnp.bfloat16)
    half = block_diag.shape[1]
    quarters = (
        (0, 0, block_diag[0]),
        (0, half, block_above[0]),
        (half, 0, block_below[1]),
        (half, half, block_diag[1]),
    )
    for first_row, first_column, block in quarters:
        place = (pl.ds(first_row, half), pl.ds(first_column, half))
        high[place], low[place] = halves(block)


def pencil_kernel(
    levels,
    velocity,
    viscosity,
    middle,
    inner,
    outer,
    blocks_high,
    blocks_low,
    lines_of,
    out,
    work,
):
    radial = work.shape[1]
    devices = radial // levels
    row, group, place = places()
    x = (group - lax.axis_index("lat")) & (ROWS - 1)
    own_lane = row * WIDTH + place

    odd = lax.axis_index("sec") & 1
    inner_x, outer_x = x == (1 - odd) * (ROWS - 1), x == odd * (ROWS - 1)

    def side(kind, start):
        near = along_row(jnp.broadcast_to(inner[kind, pl.ds(start // ROWS, 1), :], (ROWS, LANES)), own_lane)
        far = along_row(jnp.broadcast_to(outer[kind, pl.ds(start // ROWS, 1), :], (ROWS, LANES)), own_lane)
        return jnp.where(inner_x, near, jnp.where(outer_x, far, 0.0))

    for start in range(0, radial, ROWS):
        here = pl.ds(start, ROWS)
        v = velocity[pl.ds(ROWS + start, ROWS), :]
        eta = viscosity[pl.ds(ROWS + start, ROWS), :]
        v_rim = side(0, start)
        eta_rim = side(1, start)
        value_sum = middle[0, here, :] + v_rim
        eta_sum = middle[1, here, :] + eta_rim
        product_sum = middle[2, here, :] + v_rim * eta_rim
        spread = 6.0 * v - value_sum
        sensitivity = 0.5 * eta * spread
        work[0, here, :] = sensitivity + 0.5 * (v * eta_sum - product_sum) + middle[4, here, :]
        work[1, here, :] = 0.5 * eta_sum + 0.5 * middle[3, here, :] * spread + middle[5, here, :]
        work[2, here, :] = sensitivity

    residual = work[0]
    whole = ((1,), (0,))

    def apply_blocks(field):
        high, low = halves(field)
        wide = product(blocks_high[...], jnp.concatenate([high, low], axis=1), whole)
        return wide[:, :LANES] + (wide[:, LANES:] + product(blocks_low[...], high, whole))

    initial = apply_blocks(residual)
    level_index = lax.broadcasted_iota(jnp.int32, (radial, LANES), 0)
    from_above = jnp.where(level_index == radial - 1, 0.0, pltpu.roll(middle[6] * initial, radial - 1, 0))
    from_below = jnp.where(level_index == 0, 0.0, pltpu.roll(middle[7] * initial, 1, 0))
    remainder = residual - (work[1] * initial + from_above + from_below)
    correction = initial + apply_blocks(remainder)
    gradient = correction * work[2]
    high, low = halves(gradient)
    over_lines = ((1,), (1,))
    twice = jnp.concatenate([lines_of[...], lines_of[...]], axis=1)
    owned = product(twice, jnp.concatenate([high, low], axis=1), over_lines)
    work[0] = correction
    parts = radial // LANES
    back = levels + parts
    for block in range(devices // ROWS):
        for level in range(levels):
            out[pl.ds(block * ROWS * back + level, ROWS, stride=back), :] = work[
                0, pl.ds(block * ROWS * levels + level, ROWS, stride=levels), :
            ]
        for part in range(parts):
            out[pl.ds(block * ROWS * back + levels + part, ROWS, stride=back), :] = owned[
                block * ROWS : (block + 1) * ROWS, part * LANES : (part + 1) * LANES
            ]


def owned_kernel(levels, received, owned):
    sectors, _, radial = owned.shape
    parts = radial // LANES
    back = levels + parts
    blocks = received.shape[0] // (back * ROWS)
    for part in range(parts):
        total = received[pl.ds(levels + part, ROWS, stride=back), :]
        for block in range(1, blocks):
            total = total + received[pl.ds(block * ROWS * back + levels + part, ROWS, stride=back), :]
        total = jnp.sum(total, axis=0, keepdims=True)
        for sector in range(sectors):
            owned[sector, :, part * LANES : (part + 1) * LANES] = total


def finish_kernel(received, correction):
    levels, rows, width = correction.shape
    blocks = width // LANES
    back = received.shape[0] // (blocks * ROWS)
    row, group, place = places()
    row_of = (group - row) & (ROWS - 1)
    lane_of = ((group + row) & (ROWS - 1)) * WIDTH + place
    for level in range(levels):
        for block in range(blocks):
            lines = received[pl.ds(block * ROWS * back + level, ROWS, stride=back), :]
            correction[level, :, block * LANES : (block + 1) * LANES] = along_row(
                along_lane(lines, row_of), lane_of
            )


def swapped(rows, parts):
    devices = lax.axis_size("lat")
    sent = rows.reshape(devices, -1, parts, LANES)
    taken = lax.all_to_all(sent, "lat", split_axis=0, concat_axis=0, tiled=True)
    return taken.reshape(rows.shape)


def kernel_call(body, shapes, specs, work, name, scratch=()):
    return pl.pallas_call(
        body,
        out_shape=shapes,
        in_specs=specs,
        out_specs=[VMEM] * len(shapes),
        scratch_shapes=scratch,
        compiler_params=pltpu.CompilerParams(vmem_limit_bytes=32 * MIB),
        cost_estimate=pl.CostEstimate(flops=work[0], bytes_accessed=4 * work[1], transcendentals=0),
        name=name,
    )


def f32(*shape):
    return jax.ShapeDtypeStruct(shape, jnp.float32)


def local(
    velocity,
    base_visc,
    yielded,
    colors,
    forcing,
    block_diag,
    block_below,
    block_above,
    weak_lines,
    weak_owner,
):
    levels, rows, width = velocity.shape
    devices = lax.axis_size("lat")
    sectors = lax.axis_size("sec")
    radial = levels * devices
    cell_count = levels * rows * width
    tile = (levels, rows, width)
    sent_rows = FIELDS * levels + 1
    far = [
        pltpu.with_memory_space_constraint(array, pltpu.HBM)
        for array in (velocity, base_visc, yielded, colors, forcing)
    ]
    (lines,) = kernel_call(
        tile_kernel,
        [f32(devices * sent_rows, LANES)],
        [HBM] * FIELDS,
        (40 * cell_count, 12 * cell_count),
        "tile",
        [pltpu.VMEM(tile, array.dtype) for array in far] + [pltpu.SemaphoreType.DMA((FIELDS,))],
    )(*far)
    lines = swapped(lines, 1)

    def b16(*shape):
        return jax.ShapeDtypeStruct(shape, jnp.bfloat16)

    lines_of, blocks_high, blocks_low = kernel_call(
        lines_kernel,
        [b16(devices, LANES), b16(radial, radial), b16(radial, radial)],
        [VMEM] * 5,
        (2 * devices * LANES * 64, 3 * radial * radial),
        "lines",
    )(weak_lines.reshape(1, -1), weak_owner.reshape(1, -1), block_diag, block_below, block_above)
    back = levels + radial // LANES
    padded = f32(radial + 2 * ROWS, LANES)
    whole = f32(radial, LANES)
    edge = f32(2, radial // ROWS, LANES)

    def edge_body(*refs):
        edge_kernel(levels, *refs)

    def middle_body(*refs):
        middle_kernel(levels, *refs)

    def pencil_body(*refs):
        pencil_kernel(levels, *refs)

    v, eta, base, coef, inner_edge, outer_edge = kernel_call(
        edge_body,
        [padded, padded, whole, whole, edge, edge],
        [VMEM],
        (10 * cell_count, 7 * cell_count),
        "edges",
    )(lines)
    inner = lax.ppermute(inner_edge, "sec", [(i, i ^ 1) for i in range(sectors)])
    outer = lax.ppermute(outer_edge, "sec", [(i, i + 1 if i % 2 else i - 1) for i in range(1, sectors - 1)])
    (middle,) = kernel_call(
        middle_body,
        [f32(8, radial, LANES)],
        [VMEM] * 5,
        (60 * cell_count, 14 * cell_count),
        "middle",
        [pltpu.VMEM((radial, LANES), jnp.float32), pltpu.VMEM((radial, LANES), jnp.float32)],
    )(lines, v, eta, base, coef)
    (improved,) = kernel_call(
        pencil_body,
        [f32(devices * back, LANES)],
        [VMEM] * 8,
        (24 * radial * radial * LANES, 12 * radial * LANES),
        "pencil",
        [pltpu.VMEM((3, radial, LANES), jnp.float32)],
    )(v, eta, middle, inner, outer, blocks_high, blocks_low, lines_of)
    improved = swapped(improved, 2)

    def owned_body(*refs):
        owned_kernel(levels, *refs)

    (owned,) = kernel_call(
        owned_body, [f32(sectors, 1, radial)], [VMEM], (devices * radial, devices * radial), "owned"
    )(improved)
    sums = lax.all_to_all(owned, "sec", split_axis=0, concat_axis=0, tiled=True)
    (correction,) = kernel_call(
        finish_kernel, [f32(*tile)], [VMEM], (4 * cell_count, 3 * cell_count), "finish"
    )(improved)
    weak_grad = jnp.sum(sums, axis=0)
    return (correction, weak_grad)


def solution(mesh):
    return jax.shard_map(
        local,
        mesh=mesh,
        in_specs=(
            P("lat", "sec", None),
            P("lat", "sec", None),
            P("lat", "sec", None),
            P("lat", "sec", None),
            P("lat", "sec", None),
            P(),
            P(),
            P(),
            P("sec", "lat", None),
            P("sec", "lat", None, None),
        ),
        out_specs=(P("lat", "sec", None), P("lat", None)),
        check_vma=False,
    )
```
